32 devices in a mesh: ctx: 8 (over z, x), kvh: 4 (over y, core).
Axes of the slice: x: 2, y: 2, z: 4, core: 2. Of those that a mesh axis runs over, the one named last changes fastest.
Arguments:
- queries: bfloat16 [3072, 4096], P('ctx', 'kvh'), may hold values from -110 to 110
- keys: bfloat16 [3072, 1024], P('ctx', 'kvh'), may hold values from -4.5 to 4.5
- values: bfloat16 [3072, 1024], P('ctx', 'kvh'), may hold values from -6 to 6
- vertical: int32 [8, 4], P('kvh'), may hold values from 0 to 47, as said below
- offsets: int32 [8, 3], P('kvh'), may hold values from 0 to 319, as said below
Outputs:
- attended: bfloat16 [3072, 4096], P(('ctx', 'kvh'))
The draws below stay inside these ranges and needn't reach their ends.
Inputs may be any that keep to these rules, and one draw needn't show every extreme that they name: `vertical`: each entry names a block of 64 keys; the 4 blocks of one key-value head lie in distinct shards of 384 positions. `offsets`: entry 0 of every head is 0; the bands [o, o + 64) of one head are disjoint.
All inputs are finite; a program needn't handle non-finite values.
Results may differ from the reference program's by a relative error of at most 0.0044.
Values may be sent and summed in bfloat16 or wider, within the bound.
A program may use at most 128 MiB of HBM per device.

```python
import jax
import jax.numpy as jnp
from jax import lax

HD = 128
QH = 32
KVH = 8
BLK = 64
NVB = 4
NS = 3
TOK_DEV = 384
TOKENS = 3072
N_CTX = 8


def shared_draw(key):
    base = jax.random.truncated_normal(key, -4.5, 4.5, (TOKENS, KVH * HD), jnp.float32)
    return base


def draw_keys(key, part):
    base = shared_draw(key)
    result = base
    return result.astype(jnp.bfloat16)


def draw_queries(key, part):
    key = jax.random.fold_in(key, 5)
    result = jax.random.truncated_normal(key, -4.5, 4.5, (TOKENS, QH * HD), jnp.float32)
    return result.astype(jnp.bfloat16)


def draw_vertical(key, part):
    key = jax.random.fold_in(key, 7)
    per_shard = TOK_DEV // BLK
    shard_count = TOKENS // TOK_DEV

    def one_head(head_key):
        owners = jax.random.permutation(head_key, shard_count)[:NVB]
        inside = jax.random.randint(jax.random.fold_in(head_key, 1), (NVB,), 0, per_shard)
        return owners * per_shard + inside
    return jax.vmap(one_head)(jax.random.split(key, KVH)).astype(jnp.int32)


def draw_offsets(key, part):
    key = jax.random.fold_in(key, 9)
    spread = TOK_DEV // BLK - 2

    def one_head(head_key):
        picks = jax.random.permutation(head_key, spread)[:NS - 1] + 1
        jitter = jax.random.randint(jax.random.fold_in(head_key, 1), (), 0, BLK)
        return jnp.concatenate([jnp.zeros((1,), jnp.int32), (picks * BLK + jitter).astype(jnp.int32)])
    return jax.vmap(one_head)(jax.random.split(key, KVH)).astype(jnp.int32)


def level_of(key, extent, cuts, least, top_value):
    def one(position, parts):
        draws = jax.random.uniform(jax.random.fold_in(jax.random.fold_in(key, 6), position), (parts,), jnp.float32, least / len(cuts), top_value / len(cuts))
        return jnp.repeat(jnp.exp(draws), extent[position] // parts).reshape((-1,) + (1,) * (len(extent) - position - 1))

    loudness = one(*cuts[0])
    for cut in cuts[1:]:
        loudness = loudness * one(*cut)
    return loudness


def bell_draw(key, shape, width, reach, pieces=(), held_as=jnp.bfloat16):
    level = level_of(key, shape, pieces, -0.22, 0.18) if pieces else 1.0
    values = jax.random.normal(key, shape, jnp.float32) * width * level
    return jnp.minimum(jnp.maximum(values, -reach), reach).astype(held_as)


def setup_inputs(seed: int = 0) -> dict:
    seeds = jax.random.split(jax.random.key(seed), 6)
    return {
        "queries": draw_queries(jax.random.fold_in(seeds[5], 71), 0),
        "keys": draw_keys(jax.random.fold_in(seeds[5], 71), 0),
        "values": bell_draw(seeds[2], (TOKENS, KVH * HD), 1.0, 6.0, ((0, 8), (1, 4))),
        "vertical": draw_vertical(jax.random.fold_in(seeds[5], 71), 0),
        "offsets": draw_offsets(jax.random.fold_in(seeds[5], 71), 0),
    }


NEG = -1e30


def band_tiles(window, begin, tok_rows, head_width):
    tile_count = tok_rows // BLK
    section = lax.dynamic_slice_in_dim(window, begin, tok_rows + BLK, 0)
    lower = section[:tok_rows].reshape(tile_count, BLK, head_width)
    upper = section[BLK:].reshape(tile_count, BLK, head_width)
    return jnp.concatenate([lower, upper], axis=1)


def attend(query_tile, first_pos, key_window, value_window, vert_keys, vert_values, vert_blocks, band_starts):
    tok_rows, group_size, head_width = query_tile.shape
    tile_count = tok_rows // BLK
    scaling = head_width ** -0.5
    query_pos = first_pos + jnp.arange(tok_rows, dtype=jnp.int32)
    vert_pos = (vert_blocks[:, None] * BLK + jnp.arange(BLK, dtype=jnp.int32)[None, :]).reshape(-1)
    distance = query_pos[:, None] - vert_pos[None, :]
    allowed = distance >= 0
    band_count = band_starts.shape[0]
    for band_num in range(band_count):
        shifted = distance - band_starts[band_num]
        allowed = allowed & ~((shifted >= 0) & (shifted < BLK))
    query_f = query_tile.astype(jnp.float32)
    vert_scores = jnp.einsum('qgd,kd->gqk', query_f, vert_keys.astype(jnp.float32)) * scaling
    vert_scores = jnp.where(allowed[None], vert_scores, NEG)
    begins = tok_rows - band_starts - BLK
    slash_keys = jnp.stack([band_tiles(key_window, begins[b], tok_rows, head_width) for b in range(band_count)])
    slash_values = jnp.stack([band_tiles(value_window, begins[b], tok_rows, head_width) for b in range(band_count)])
    query_blocks = query_f.reshape(tile_count, BLK, group_size, head_width)
    slash_scores = jnp.einsum('tagd,stcd->gstac', query_blocks, slash_keys.astype(jnp.float32)) * scaling
    lag_rows = jnp.arange(BLK, dtype=jnp.int32)[:, None] + BLK - jnp.arange(2 * BLK, dtype=jnp.int32)[None, :]
    key_pos = query_pos.reshape(tile_count, BLK)[None, :, :, None] - band_starts[:, None, None, None] - lag_rows[None, None]
    band_mask = (lag_rows >= 0)[None, None] & (lag_rows < BLK)[None, None] & (key_pos >= 0)
    slash_scores = jnp.where(band_mask[None], slash_scores, NEG)
    row_top = jnp.maximum(vert_scores.max(axis=-1), slash_scores.max(axis=(1, 4)).reshape(group_size, tok_rows))
    vert_exp = jnp.exp(vert_scores - row_top[:, :, None])
    slash_exp = jnp.exp(slash_scores - row_top.reshape(group_size, tile_count, BLK)[:, None, :, :, None])
    totals = vert_exp.sum(axis=-1) + slash_exp.sum(axis=(1, 4)).reshape(group_size, tok_rows)
    vert_weights = lax.optimization_barrier(vert_exp.astype(jnp.bfloat16)).astype(jnp.float32)
    slash_weights = lax.optimization_barrier(slash_exp.astype(jnp.bfloat16)).astype(jnp.float32)
    blended = jnp.einsum('gqk,kd->qgd', vert_weights, vert_values.astype(jnp.float32))
    blended = blended + jnp.einsum('gstac,stcd->tagd', slash_weights, slash_values.astype(jnp.float32)).reshape(tok_rows, group_size, head_width)
    result = blended / totals.T[:, :, None]
    return result.astype(jnp.bfloat16).reshape(tok_rows, group_size * head_width)


def reference(queries, keys, values, vertical, offsets):
    tokens = queries.shape[0]
    kv_total = vertical.shape[0]
    head_width = keys.shape[1] // kv_total
    group_size = queries.shape[1] // keys.shape[1]

    def per_head(head_num):
        key_col = lax.dynamic_slice_in_dim(keys, head_num * head_width, head_width, 1)
        value_col = lax.dynamic_slice_in_dim(values, head_num * head_width, head_width, 1)
        padding = jnp.zeros((TOK_DEV, head_width), jnp.bfloat16)
        key_pad = jnp.concatenate([padding, key_col], axis=0)
        value_pad = jnp.concatenate([padding, value_col], axis=0)
        vert_blocks = vertical[head_num]
        band_starts = offsets[head_num]
        vert_pos = (vert_blocks[:, None] * BLK + jnp.arange(BLK, dtype=jnp.int32)[None, :]).reshape(-1)
        vert_keys = key_col[vert_pos]
        vert_values = value_col[vert_pos]

        def per_block(block_num):
            first_pos = (block_num * TOK_DEV).astype(jnp.int32)
            query_tile = lax.dynamic_slice(queries, (first_pos, (head_num * group_size * head_width).astype(jnp.int32)), (TOK_DEV, group_size * head_width))
            query_tile = query_tile.reshape(TOK_DEV, group_size, head_width)
            key_window = lax.dynamic_slice_in_dim(key_pad, first_pos, 2 * TOK_DEV, 0)
            value_window = lax.dynamic_slice_in_dim(value_pad, first_pos, 2 * TOK_DEV, 0)
            return attend(query_tile, first_pos, key_window, value_window, vert_keys, vert_values, vert_blocks, band_starts)

        return lax.map(per_block, jnp.arange(N_CTX, dtype=jnp.int32))

    stacked = lax.map(per_head, jnp.arange(kv_total, dtype=jnp.int32))
    return stacked.transpose(1, 2, 0, 3).reshape(tokens, queries.shape[1])
```

```python
import functools
import math

import jax
import jax.numpy as jnp
from jax import lax
from jax.experimental import pallas as pl
from jax.experimental.pallas import tpu as pltpu
from jax.sharding import PartitionSpec as P

BLK = 64
NEG = -1e30
MESH = pl.DeviceIdType.MESH


def each(count, body):
    if count <= 16:
        for i in range(count):
            body(i)
    else:
        lax.fori_loop(0, count, lambda i, carry: (body(i), carry)[1], 0)


def kernel(
    n_ctx,
    n_kvh,
    vert_ref,
    offs_ref,
    q_ref,
    k_ref,
    v_ref,
    out_ref,
    k_prev,
    v_prev,
    gath,
    obuf,
    kv_send,
    kv_recv,
    vert_send,
    vert_recv,
    out_send,
    out_recv,
    out_local,
):
    c = lax.axis_index("ctx")
    me = lax.axis_index("kvh")
    tok = q_ref.shape[0]
    heads = vert_ref.shape[0]
    slots = vert_ref.shape[1]
    bands = offs_ref.shape[1]
    hd = k_ref.shape[1] // heads
    group = q_ref.shape[1] // k_ref.shape[1]
    gcols = group * hd
    rows = tok // n_kvh
    span = rows + tok
    per_shard = tok // BLK

    def ctx_peer(i):
        return lax.rem(c + 1 + i, n_ctx)

    barrier = pltpu.get_barrier_semaphore()
    each(
        n_ctx - 1,
        lambda i: pl.semaphore_signal(
            barrier, inc=1, device_id={"ctx": ctx_peer(i)}, device_id_type=MESH
        ),
    )
    for i in range(n_kvh - 1):
        pl.semaphore_signal(
            barrier,
            inc=1,
            device_id={"kvh": lax.rem(me + 1 + i, n_kvh)},
            device_id_type=MESH,
        )

    for g in range(heads):
        row = jnp.int32(0)
        for j in range(slots):
            block = vert_ref[g, j]
            away = lax.div(block, per_shard) - c
            row = row + lax.rem(block, per_shard) * (1 - jnp.minimum(away * away, 1))
        row = row * BLK
        cols = slice(g * hd, (g + 1) * hd)
        gath[c, g, 0] = k_ref[pl.ds(row, BLK), cols]
        gath[c, g, 1] = v_ref[pl.ds(row, BLK), cols]

    pl.semaphore_wait(barrier, n_ctx - 1 + n_kvh - 1)

    def vert_copy(i):
        peer = ctx_peer(i)
        return pltpu.make_async_remote_copy(
            src_ref=gath.at[c],
            dst_ref=gath.at[c],
            send_sem=vert_send.at[peer],
            recv_sem=vert_recv.at[c],
            device_id={"ctx": peer},
            device_id_type=MESH,
        )

    def vert_arrival(i):
        peer = ctx_peer(i)
        return pltpu.make_async_remote_copy(
            src_ref=gath.at[peer],
            dst_ref=gath.at[peer],
            send_sem=vert_send.at[peer],
            recv_sem=vert_recv.at[peer],
            device_id={"ctx": peer},
            device_id_type=MESH,
        )

    def kv_copy(which, chunk):
        src, dst = ((k_ref, k_prev), (v_ref, v_prev))[which]
        part = pl.ds(chunk * rows, rows)
        return pltpu.make_async_remote_copy(
            src_ref=src.at[part],
            dst_ref=dst.at[part],
            send_sem=kv_send.at[which, chunk],
            recv_sem=kv_recv.at[which, chunk],
            device_id={"ctx": lax.rem(c + 1, n_ctx)},
            device_id_type=MESH,
        )

    each(n_ctx - 1, lambda i: vert_copy(i).start())

    @pl.when(c < n_ctx - 1)
    def _():
        for chunk in reversed(range(n_kvh)):
            for which in range(2):
                kv_copy(which, chunk).start()

    @pl.when(c == 0)
    def _():
        k_prev[...] = jnp.zeros_like(k_prev)
        v_prev[...] = jnp.zeros_like(v_prev)

    lag = (
        lax.broadcasted_iota(jnp.int32, (rows, span), 0)
        + tok
        - lax.broadcasted_iota(jnp.int32, (rows, span), 1)
    )
    window_col = lax.broadcasted_iota(jnp.int32, (rows, span), 1)
    vert_lane = lax.broadcasted_iota(jnp.int32, (1, slots * BLK), 1)
    vert_row = lax.broadcasted_iota(jnp.int32, (rows, slots * BLK), 0)

    def in_bands(distance, g):
        found = None
        for s in range(bands):
            gap = distance - offs_ref[g, s]
            hit = (gap >= 0) & (gap < BLK)
            found = hit if found is None else found | hit
        return found

    each(n_ctx - 1, lambda i: vert_arrival(i).wait_recv())

    vert_k, vert_v, vert_pos = [], [], []
    for g in range(heads):
        owners = [lax.div(vert_ref[g, j], per_shard) for j in range(slots)]
        vert_k.append(jnp.concatenate([gath[o, g, 0] for o in owners], axis=0))
        vert_v.append(jnp.concatenate([gath[o, g, 1] for o in owners], axis=0))
        first = jnp.zeros_like(vert_lane)
        for j in range(slots):
            first = jnp.where(vert_lane // BLK == j, vert_ref[g, j], first)
        vert_pos.append(first * BLK + vert_lane % BLK)

    factor = math.log2(math.e) * hd**-0.5

    def out_copy(tile, g):
        return pltpu.make_async_remote_copy(
            src_ref=obuf.at[pl.ds(tile * rows, rows), pl.ds(g * gcols, gcols)],
            dst_ref=out_ref.at[
                :, pl.ds(pl.multiple_of(me * heads * gcols + g * gcols, gcols), gcols)
            ],
            send_sem=out_send.at[tile, g],
            recv_sem=out_recv.at[me, g],
            device_id={"kvh": tile},
            device_id_type=MESH,
        )

    def out_own(tile, g):
        return pltpu.make_async_copy(
            obuf.at[pl.ds(tile * rows, rows), pl.ds(g * gcols, gcols)],
            out_ref.at[
                :, pl.ds(pl.multiple_of(me * heads * gcols + g * gcols, gcols), gcols)
            ],
            out_local.at[g],
        )

    def out_arrival(peer, g):
        return pltpu.make_async_remote_copy(
            src_ref=obuf.at[pl.ds(0, rows), pl.ds(g * gcols, gcols)],
            dst_ref=out_ref.at[:, pl.ds(peer * heads * gcols + g * gcols, gcols)],
            send_sem=out_send.at[peer, g],
            recv_sem=out_recv.at[peer, g],
            device_id={"kvh": peer},
            device_id_type=MESH,
        )

    for tile in reversed(range(n_kvh)):
        base = tile * rows

        @pl.when(c > 0)
        def _():
            for which in range(2):
                kv_copy(which, tile).wait_recv()

        before = jnp.where(c == 0, tok - base, 0)
        for g in range(heads):
            cols = slice(g * hd, (g + 1) * hd)
            q = jnp.concatenate(
                [
                    q_ref[base : base + rows, (g * group + h) * hd : (g * group + h + 1) * hd]
                    for h in range(group)
                ],
                axis=0,
            )
            keys = jnp.concatenate([k_prev[base:, cols], k_ref[: base + rows, cols]], axis=0)
            vals = jnp.concatenate([v_prev[base:, cols], v_ref[: base + rows, cols]], axis=0)
            dims = (((1,), (1,)), ((), ()))
            score_w = lax.dot_general(q, keys, dims, preferred_element_type=jnp.float32)
            score_v = lax.dot_general(q, vert_k[g], dims, preferred_element_type=jnp.float32)
            mask_w = in_bands(lag, g) & (window_col >= before)
            vert_lag = vert_row + (c * tok + base) - vert_pos[g]
            mask_v = (vert_lag >= 0) & ~in_bands(vert_lag, g)
            score_w = jnp.where(mask_w[None], score_w.reshape(group, rows, span), NEG)
            score_v = jnp.where(mask_v[None], score_v.reshape(group, rows, slots * BLK), NEG)
            top = jnp.maximum(
                jnp.max(score_w, axis=-1, keepdims=True), jnp.max(score_v, axis=-1, keepdims=True)
            )
            exp_w = jnp.exp2((score_w - top) * factor)
            exp_v = jnp.exp2((score_v - top) * factor)
            total = jnp.sum(exp_w, axis=-1, keepdims=True) + jnp.sum(exp_v, axis=-1, keepdims=True)
            blended = jnp.dot(
                exp_w.astype(jnp.bfloat16).reshape(group * rows, span),
                vals,
                preferred_element_type=jnp.float32,
            ) + jnp.dot(
                exp_v.astype(jnp.bfloat16).reshape(group * rows, slots * BLK),
                vert_v[g],
                preferred_element_type=jnp.float32,
            )
            result = (blended.reshape(group, rows, hd) / total).astype(jnp.bfloat16)
            for h in range(group):
                obuf[base : base + rows, (g * group + h) * hd : (g * group + h + 1) * hd] = result[h]

            @pl.when(tile != me)
            def _():
                out_copy(tile, g).start()

            @pl.when(tile == me)
            def _():
                out_own(tile, g).start()

    each(n_ctx - 1, lambda i: vert_copy(i).wait_send())

    @pl.when(c < n_ctx - 1)
    def _():
        for chunk in range(n_kvh):
            for which in range(2):
                kv_copy(which, chunk).wait_send()

    for peer in range(n_kvh):
        for g in range(heads):

            @pl.when(peer != me)
            def _():
                out_copy(peer, g).wait_send()
                out_arrival(peer, g).wait_recv()

            @pl.when(peer == me)
            def _():
                out_own(peer, g).wait()


def per_device(n_ctx, n_kvh, queries, keys, values, vertical, offsets):
    tok = queries.shape[0]
    heads = vertical.shape[0]
    hd = keys.shape[1] // heads
    rows = tok // n_kvh
    vmem = pl.BlockSpec(memory_space=pltpu.VMEM)
    smem = pl.BlockSpec(memory_space=pltpu.SMEM)
    dma = pltpu.SemaphoreType.DMA
    return pl.pallas_call(
        functools.partial(kernel, n_ctx, n_kvh),
        out_shape=jax.ShapeDtypeStruct((rows, queries.shape[1] * n_kvh), jnp.bfloat16),
        in_specs=[smem, smem, vmem, vmem, vmem],
        out_specs=pl.BlockSpec(memory_space=pl.ANY),
        scratch_shapes=[
            pltpu.VMEM(keys.shape, jnp.bfloat16),
            pltpu.VMEM(values.shape, jnp.bfloat16),
            pltpu.VMEM((n_ctx, heads, 2, BLK, hd), jnp.bfloat16),
            pltpu.VMEM(queries.shape, jnp.bfloat16),
            dma((2, n_kvh)),
            dma((2, n_kvh)),
            dma((n_ctx,)),
            dma((n_ctx,)),
            dma((n_kvh, heads)),
            dma((n_kvh, heads)),
            dma((heads,)),
        ],
        compiler_params=pltpu.CompilerParams(
            collective_id=0, has_side_effects=True, vmem_limit_bytes=48 * 1024 * 1024
        ),
    )(vertical, offsets, queries, keys, values)


def solution(mesh):
    placed = (P("ctx", "kvh"), P("ctx", "kvh"), P("ctx", "kvh"), P("kvh", None), P("kvh", None))
    return jax.shard_map(
        functools.partial(per_device, mesh.shape["ctx"], mesh.shape["kvh"]),
        mesh=mesh,
        in_specs=placed,
        out_specs=P(("ctx", "kvh"), None),
        check_vma=False,
    )
```

```python
import functools
import math

import jax
import jax.numpy as jnp
from jax import lax
from jax.experimental import pallas as pl
from jax.experimental.pallas import tpu as pltpu
from jax.sharding import PartitionSpec as P

BLK = 64
NEG = -1e30
MESH = pl.DeviceIdType.MESH


def each(count, body):
    if count <= 16:
        for i in range(count):
            body(i)
    else:
        lax.fori_loop(0, count, lambda i, carry: (body(i), carry)[1], 0)


def kernel(
    n_ctx,
    n_kvh,
    vert_hbm,
    offs_hbm,
    q_hbm,
    k_hbm,
    v_hbm,
    out_ref,
    vert_ref,
    offs_ref,
    q_ref,
    k_ref,
    v_ref,
    k_prev,
    v_prev,
    gath,
    obuf,
    kv_send,
    kv_recv,
    pair_send,
    pair_recv,
    chain_send,
    chain_recv,
    out_send,
    out_recv,
    out_local,
    load_sem,
):
    c = lax.axis_index("ctx")
    me = lax.axis_index("kvh")
    tok = q_ref.shape[0]
    heads = vert_ref.shape[0]
    slots = vert_ref.shape[1]
    bands = offs_ref.shape[1]
    hd = k_ref.shape[1] // heads
    group = q_ref.shape[1] // k_ref.shape[1]
    gcols = group * hd
    rows = tok // n_kvh
    span = rows + tok
    per_shard = tok // BLK

    z, x = c // 2, c % 2
    n_z = n_ctx // 2
    partner = c + 1 - 2 * x

    loads = [
        pltpu.make_async_copy(src, dst, load_sem.at[i])
        for i, (src, dst) in enumerate(
            (
                (vert_hbm, vert_ref),
                (offs_hbm, offs_ref),
                (k_hbm, k_ref),
                (v_hbm, v_ref),
                (q_hbm, q_ref),
            )
        )
    ]
    for load in loads:
        load.start()

    barrier = pltpu.get_barrier_semaphore()
    for step in (1, -1, 2, -2):

        @pl.when((c + step >= 0) & (c + step < n_ctx))
        def _():
            pl.semaphore_signal(
                barrier, inc=1, device_id={"ctx": c + step}, device_id_type=MESH
            )

    for i in range(n_kvh - 1):
        pl.semaphore_signal(
            barrier,
            inc=1,
            device_id={"kvh": lax.rem(me + 1 + i, n_kvh)},
            device_id_type=MESH,
        )
    greeted = jnp.minimum(c, 2) + jnp.minimum(n_ctx - 1 - c, 2) + n_kvh - 1

    for load in loads[:4]:
        load.wait()

    for g in range(heads):
        row = jnp.int32(0)
        for j in range(slots):
            block = vert_ref[g, j]
            away = lax.div(block, per_shard) - c
            row = row + lax.rem(block, per_shard) * (1 - jnp.minimum(away * away, 1))
        row = row * BLK
        cols = slice(g * hd, (g + 1) * hd)
        gath[c, g, 0] = k_ref[pl.ds(row, BLK), cols]
        gath[c, g, 1] = v_ref[pl.ds(row, BLK), cols]

    pl.semaphore_wait(barrier, greeted)

    pair_copy = pltpu.make_async_remote_copy(
        src_ref=gath.at[c],
        dst_ref=gath.at[c],
        send_sem=pair_send,
        recv_sem=pair_recv,
        device_id={"ctx": partner},
        device_id_type=MESH,
    )

    def chain_copy(pair, step):
        part = gath.at[pl.ds(2 * pair, 2)]
        return pltpu.make_async_remote_copy(
            src_ref=part,
            dst_ref=part,
            send_sem=chain_send.at[(step + 1) // 2, pair],
            recv_sem=chain_recv.at[pair],
            device_id={"ctx": c + 2 * step},
            device_id_type=MESH,
        )

    def chain_round(i):
        for step in (1, -1):
            pair = z - step * i
            there = (pair >= 0) & (pair < n_z)
            onward = (z + step >= 0) & (z + step < n_z)
            if not isinstance(i, int) or i > 0:

                @pl.when(there)
                def _():
                    chain_copy(pair, step).wait_recv()

            @pl.when(there & onward)
            def _():
                chain_copy(pair, step).start()

    def chain_sent(i):
        for step in (1, -1):
            pair = z - step * i
            there = (pair >= 0) & (pair < n_z)
            onward = (z + step >= 0) & (z + step < n_z)

            @pl.when(there & onward)
            def _():
                chain_copy(pair, step).wait_send()

    def kv_copy(which, chunk):
        src, dst = ((k_hbm, k_prev), (v_hbm, v_prev))[which]
        part = pl.ds(chunk * rows, rows)
        return pltpu.make_async_remote_copy(
            src_ref=src.at[part],
            dst_ref=dst.at[part],
            send_sem=kv_send.at[which, chunk],
            recv_sem=kv_recv.at[which, chunk],
            device_id={"ctx": lax.rem(c + 1, n_ctx)},
            device_id_type=MESH,
        )

    pair_copy.start()

    @pl.when(c < n_ctx - 1)
    def _():
        for chunk in reversed(range(n_kvh)):
            for which in range(2):
                kv_copy(which, chunk).start()

    pair_copy.wait_recv()
    chain_round(0)

    @pl.when(c == 0)
    def _():
        k_prev[...] = jnp.zeros_like(k_prev)
        v_prev[...] = jnp.zeros_like(v_prev)

    lag = (
        lax.broadcasted_iota(jnp.int32, (rows, span), 0)
        + tok
        - lax.broadcasted_iota(jnp.int32, (rows, span), 1)
    )
    window_col = lax.broadcasted_iota(jnp.int32, (rows, span), 1)
    vert_lane = lax.broadcasted_iota(jnp.int32, (1, slots * BLK), 1)
    vert_row = lax.broadcasted_iota(jnp.int32, (rows, slots * BLK), 0)

    def in_bands(distance, g):
        found = None
        for s in range(bands):
            gap = distance - offs_ref[g, s]
            hit = (gap >= 0) & (gap < BLK)
            found = hit if found is None else found | hit
        return found

    each(n_z - 1, lambda i: chain_round(i + 1))
    loads[4].wait()

    vert_k, vert_v, vert_pos = [], [], []
    for g in range(heads):
        owners = [lax.div(vert_ref[g, j], per_shard) for j in range(slots)]
        vert_k.append(jnp.concatenate([gath[o, g, 0] for o in owners], axis=0))
        vert_v.append(jnp.concatenate([gath[o, g, 1] for o in owners], axis=0))
        first = jnp.zeros_like(vert_lane)
        for j in range(slots):
            first = jnp.where(vert_lane // BLK == j, vert_ref[g, j], first)
        vert_pos.append(first * BLK + vert_lane % BLK)

    factor = math.log2(math.e) * hd**-0.5

    def out_copy(tile, g):
        return pltpu.make_async_remote_copy(
            src_ref=obuf.at[pl.ds(tile * rows, rows), pl.ds(g * gcols, gcols)],
            dst_ref=out_ref.at[
                :, pl.ds(pl.multiple_of(me * heads * gcols + g * gcols, gcols), gcols)
            ],
            send_sem=out_send.at[tile, g],
            recv_sem=out_recv.at[me, g],
            device_id={"kvh": tile},
            device_id_type=MESH,
        )

    def out_own(tile, g):
        return pltpu.make_async_copy(
            obuf.at[pl.ds(tile * rows, rows), pl.ds(g * gcols, gcols)],
            out_ref.at[
                :, pl.ds(pl.multiple_of(me * heads * gcols + g * gcols, gcols), gcols)
            ],
            out_local.at[g],
        )

    def out_arrival(peer, g):
        return pltpu.make_async_remote_copy(
            src_ref=obuf.at[pl.ds(0, rows), pl.ds(g * gcols, gcols)],
            dst_ref=out_ref.at[:, pl.ds(peer * heads * gcols + g * gcols, gcols)],
            send_sem=out_send.at[peer, g],
            recv_sem=out_recv.at[peer, g],
            device_id={"kvh": peer},
            device_id_type=MESH,
        )

    for tile in reversed(range(n_kvh)):
        base = tile * rows

        @pl.when(c > 0)
        def _():
            for which in range(2):
                kv_copy(which, tile).wait_recv()

        before = jnp.where(c == 0, tok - base, 0)
        for g in range(heads):
            cols = slice(g * hd, (g + 1) * hd)
            q = jnp.concatenate(
                [
                    q_ref[base : base + rows, (g * group + h) * hd : (g * group + h + 1) * hd]
                    for h in range(group)
                ],
                axis=0,
            )
            keys = jnp.concatenate([k_prev[base:, cols], k_ref[: base + rows, cols]], axis=0)
            vals = jnp.concatenate([v_prev[base:, cols], v_ref[: base + rows, cols]], axis=0)
            dims = (((1,), (1,)), ((), ()))
            score_w = lax.dot_general(q, keys, dims, preferred_element_type=jnp.float32)
            score_v = lax.dot_general(q, vert_k[g], dims, preferred_element_type=jnp.float32)
            mask_w = in_bands(lag, g) & (window_col >= before)
            vert_lag = vert_row + (c * tok + base) - vert_pos[g]
            mask_v = (vert_lag >= 0) & ~in_bands(vert_lag, g)
            score_w = jnp.where(mask_w[None], score_w.reshape(group, rows, span), NEG)
            score_v = jnp.where(mask_v[None], score_v.reshape(group, rows, slots * BLK), NEG)
            top = jnp.maximum(
                jnp.max(score_w, axis=-1, keepdims=True), jnp.max(score_v, axis=-1, keepdims=True)
            )
            exp_w = jnp.exp2((score_w - top) * factor)
            exp_v = jnp.exp2((score_v - top) * factor)
            total = jnp.sum(exp_w, axis=-1, keepdims=True) + jnp.sum(exp_v, axis=-1, keepdims=True)
            blended = jnp.dot(
                exp_w.astype(jnp.bfloat16).reshape(group * rows, span),
                vals,
                preferred_element_type=jnp.float32,
            ) + jnp.dot(
                exp_v.astype(jnp.bfloat16).reshape(group * rows, slots * BLK),
                vert_v[g],
                preferred_element_type=jnp.float32,
            )
            result = (blended.reshape(group, rows, hd) / total).astype(jnp.bfloat16)
            for h in range(group):
                obuf[base : base + rows, (g * group + h) * hd : (g * group + h + 1) * hd] = result[h]

            @pl.when(tile != me)
            def _():
                out_copy(tile, g).start()

            @pl.when(tile == me)
            def _():
                out_own(tile, g).start()

    pair_copy.wait_send()
    each(n_z, chain_sent)

    @pl.when(c < n_ctx - 1)
    def _():
        for chunk in range(n_kvh):
            for which in range(2):
                kv_copy(which, chunk).wait_send()

    for peer in range(n_kvh):
        for g in range(heads):

            @pl.when(peer != me)
            def _():
                out_copy(peer, g).wait_send()
                out_arrival(peer, g).wait_recv()

            @pl.when(peer == me)
            def _():
                out_own(peer, g).wait()


def per_device(n_ctx, n_kvh, queries, keys, values, vertical, offsets):
    tok = queries.shape[0]
    heads = vertical.shape[0]
    hd = keys.shape[1] // heads
    rows = tok // n_kvh
    hbm = pl.BlockSpec(memory_space=pltpu.HBM)
    dma = pltpu.SemaphoreType.DMA
    return pl.pallas_call(
        functools.partial(kernel, n_ctx, n_kvh),
        out_shape=jax.ShapeDtypeStruct((rows, queries.shape[1] * n_kvh), jnp.bfloat16),
        in_specs=[hbm] * 5,
        out_specs=pl.BlockSpec(memory_space=pl.ANY),
        scratch_shapes=[
            pltpu.SMEM(vertical.shape, jnp.int32),
            pltpu.SMEM(offsets.shape, jnp.int32),
            pltpu.VMEM(queries.shape, jnp.bfloat16),
            pltpu.VMEM(keys.shape, jnp.bfloat16),
            pltpu.VMEM(values.shape, jnp.bfloat16),
            pltpu.VMEM(keys.shape, jnp.bfloat16),
            pltpu.VMEM(values.shape, jnp.bfloat16),
            pltpu.VMEM((n_ctx, heads, 2, BLK, hd), jnp.bfloat16),
            pltpu.VMEM(queries.shape, jnp.bfloat16),
            dma((2, n_kvh)),
            dma((2, n_kvh)),
            dma,
            dma,
            dma((2, n_ctx // 2)),
            dma((n_ctx // 2,)),
            dma((n_kvh, heads)),
            dma((n_kvh, heads)),
            dma((heads,)),
            dma((5,)),
        ],
        compiler_params=pltpu.CompilerParams(
            collective_id=0, has_side_effects=True, vmem_limit_bytes=64 * 1024 * 1024
        ),
    )(vertical, offsets, queries, keys, values)


def solution(mesh):
    placed = (P("ctx", "kvh"), P("ctx", "kvh"), P("ctx", "kvh"), P("kvh", None), P("kvh", None))
    return jax.shard_map(
        functools.partial(per_device, mesh.shape["ctx"], mesh.shape["kvh"]),
        mesh=mesh,
        in_specs=placed,
        out_specs=P(("ctx", "kvh"), None),
        check_vma=False,
    )
```

```python
import functools
import math

import jax
import jax.numpy as jnp
from jax import lax
from jax.experimental import pallas as pl
from jax.experimental.pallas import tpu as pltpu
from jax.sharding import PartitionSpec as P

BLK = 64
NEG = -1e30
MESH = pl.DeviceIdType.MESH


def each(count, body):
    if count <= 16:
        for i in range(count):
            body(i)
    else:
        lax.fori_loop(0, count, lambda i, carry: (body(i), carry)[1], 0)


def kernel(
    n_ctx,
    n_kvh,
    vert_hbm,
    offs_hbm,
    q_hbm,
    k_hbm,
    v_hbm,
    out_ref,
    vert_ref,
    offs_ref,
    q_ref,
    k_ref,
    v_ref,
    k_prev,
    v_prev,
    gath,
    obuf,
    kv_send,
    kv_recv,
    col_send,
    col_recv,
    relay_send,
    relay_recv,
    out_send,
    out_recv,
    out_local,
    load_sem,
):
    c = lax.axis_index("ctx")
    me = lax.axis_index("kvh")
    tok = q_ref.shape[0]
    heads = vert_ref.shape[0]
    slots = vert_ref.shape[1]
    bands = offs_ref.shape[1]
    hd = k_ref.shape[1] // heads
    group = q_ref.shape[1] // k_ref.shape[1]
    gcols = group * hd
    rows = tok // n_kvh
    span = rows + tok
    per_shard = tok // BLK

    z, x = c // 2, c % 2
    n_z = n_ctx // 2
    partner = c + 1 - 2 * x

    loads = [
        pltpu.make_async_copy(src, dst, load_sem.at[i])
        for i, (src, dst) in enumerate(
            (
                (vert_hbm, vert_ref),
                (offs_hbm, offs_ref),
                (k_hbm, k_ref),
                (v_hbm, v_ref),
                (q_hbm, q_ref),
            )
        )
    ]
    for load in loads:
        load.start()

    barrier = pltpu.get_barrier_semaphore()

    def column(i):
        return lax.rem(z + 1 + i, n_z)

    each(
        n_z - 1,
        lambda i: pl.semaphore_signal(
            barrier, inc=1, device_id={"ctx": 2 * column(i) + x}, device_id_type=MESH
        ),
    )
    for step in (1, -1):

        @pl.when((c + step >= 0) & (c + step < n_ctx))
        def _():
            pl.semaphore_signal(
                barrier, inc=1, device_id={"ctx": c + step}, device_id_type=MESH
            )

    for i in range(n_kvh - 1):
        pl.semaphore_signal(
            barrier,
            inc=1,
            device_id={"kvh": lax.rem(me + 1 + i, n_kvh)},
            device_id_type=MESH,
        )
    greeted = n_z - 1 + jnp.minimum(c, 1) + jnp.minimum(n_ctx - 1 - c, 1) + n_kvh - 1

    for load in loads[:4]:
        load.wait()

    for g in range(heads):
        row = jnp.int32(0)
        for j in range(slots):
            block = vert_ref[g, j]
            away = lax.div(block, per_shard) - c
            row = row + lax.rem(block, per_shard) * (1 - jnp.minimum(away * away, 1))
        row = row * BLK
        cols = slice(g * hd, (g + 1) * hd)
        gath[c, g, 0] = k_ref[pl.ds(row, BLK), cols]
        gath[c, g, 1] = v_ref[pl.ds(row, BLK), cols]

    pl.semaphore_wait(barrier, greeted)

    def column_copy(i):
        peer = column(i)
        return pltpu.make_async_remote_copy(
            src_ref=gath.at[c],
            dst_ref=gath.at[c],
            send_sem=col_send.at[peer],
            recv_sem=col_recv.at[z],
            device_id={"ctx": 2 * peer + x},
            device_id_type=MESH,
        )

    def column_arrival(i):
        peer = column(i)
        return pltpu.make_async_remote_copy(
            src_ref=gath.at[2 * peer + x],
            dst_ref=gath.at[2 * peer + x],
            send_sem=col_send.at[peer],
            recv_sem=col_recv.at[peer],
            device_id={"ctx": 2 * peer + x},
            device_id_type=MESH,
        )

    def relay_copy(row):
        part = gath.at[2 * row + x]
        return pltpu.make_async_remote_copy(
            src_ref=part,
            dst_ref=part,
            send_sem=relay_send.at[row],
            recv_sem=relay_recv.at[row],
            device_id={"ctx": partner},
            device_id_type=MESH,
        )

    def relay_arrival(row):
        part = gath.at[2 * row + 1 - x]
        return pltpu.make_async_remote_copy(
            src_ref=part,
            dst_ref=part,
            send_sem=relay_send.at[row],
            recv_sem=relay_recv.at[row],
            device_id={"ctx": partner},
            device_id_type=MESH,
        )

    def relay_round(i):
        column_arrival(i).wait_recv()
        relay_copy(column(i)).start()

    def kv_copy(which, chunk):
        src, dst = ((k_hbm, k_prev), (v_hbm, v_prev))[which]
        part = pl.ds(chunk * rows, rows)
        return pltpu.make_async_remote_copy(
            src_ref=src.at[part],
            dst_ref=dst.at[part],
            send_sem=kv_send.at[which, chunk],
            recv_sem=kv_recv.at[which, chunk],
            device_id={"ctx": lax.rem(c + 1, n_ctx)},
            device_id_type=MESH,
        )

    def kv_start(chunks):
        @pl.when(c < n_ctx - 1)
        def _():
            for chunk in chunks:
                for which in range(2):
                    kv_copy(which, chunk).start()

    each(n_z - 1, lambda i: column_copy(i).start())
    relay_copy(z).start()
    kv_start(range(n_kvh - 1, n_kvh // 2 - 1, -1))
    each(n_z - 1, relay_round)
    kv_start(range(n_kvh // 2 - 1, -1, -1))

    @pl.when(c == 0)
    def _():
        k_prev[...] = jnp.zeros_like(k_prev)
        v_prev[...] = jnp.zeros_like(v_prev)

    lag = (
        lax.broadcasted_iota(jnp.int32, (rows, span), 0)
        + tok
        - lax.broadcasted_iota(jnp.int32, (rows, span), 1)
    )
    window_col = lax.broadcasted_iota(jnp.int32, (rows, span), 1)
    vert_lane = lax.broadcasted_iota(jnp.int32, (1, slots * BLK), 1)
    vert_row = lax.broadcasted_iota(jnp.int32, (rows, slots * BLK), 0)

    def in_bands(distance, g):
        found = None
        for s in range(bands):
            gap = distance - offs_ref[g, s]
            hit = (gap >= 0) & (gap < BLK)
            found = hit if found is None else found | hit
        return found

    each(n_z, lambda i: relay_arrival(i).wait_recv())
    loads[4].wait()

    vert_k, vert_v, vert_pos = [], [], []
    for g in range(heads):
        owners = [lax.div(vert_ref[g, j], per_shard) for j in range(slots)]
        vert_k.append(jnp.concatenate([gath[o, g, 0] for o in owners], axis=0))
        vert_v.append(jnp.concatenate([gath[o, g, 1] for o in owners], axis=0))
        first = jnp.zeros_like(vert_lane)
        for j in range(slots):
            first = jnp.where(vert_lane // BLK == j, vert_ref[g, j], first)
        vert_pos.append(first * BLK + vert_lane % BLK)

    factor = math.log2(math.e) * hd**-0.5

    def out_copy(tile, g):
        return pltpu.make_async_remote_copy(
            src_ref=obuf.at[pl.ds(tile * rows, rows), pl.ds(g * gcols, gcols)],
            dst_ref=out_ref.at[
                :, pl.ds(pl.multiple_of(me * heads * gcols + g * gcols, gcols), gcols)
            ],
            send_sem=out_send.at[tile, g],
            recv_sem=out_recv.at[me, g],
            device_id={"kvh": tile},
            device_id_type=MESH,
        )

    def out_own(tile, g):
        return pltpu.make_async_copy(
            obuf.at[pl.ds(tile * rows, rows), pl.ds(g * gcols, gcols)],
            out_ref.at[
                :, pl.ds(pl.multiple_of(me * heads * gcols + g * gcols, gcols), gcols)
            ],
            out_local.at[g],
        )

    def out_arrival(peer, g):
        return pltpu.make_async_remote_copy(
            src_ref=obuf.at[pl.ds(0, rows), pl.ds(g * gcols, gcols)],
            dst_ref=out_ref.at[:, pl.ds(peer * heads * gcols + g * gcols, gcols)],
            send_sem=out_send.at[peer, g],
            recv_sem=out_recv.at[peer, g],
            device_id={"kvh": peer},
            device_id_type=MESH,
        )

    for tile in reversed(range(n_kvh)):
        base = tile * rows

        @pl.when(c > 0)
        def _():
            for which in range(2):
                kv_copy(which, tile).wait_recv()

        before = jnp.where(c == 0, tok - base, 0)
        for g in range(heads):
            cols = slice(g * hd, (g + 1) * hd)
            q = jnp.concatenate(
                [
                    q_ref[base : base + rows, (g * group + h) * hd : (g * group + h + 1) * hd]
                    for h in range(group)
                ],
                axis=0,
            )
            keys = jnp.concatenate([k_prev[base:, cols], k_ref[: base + rows, cols]], axis=0)
            vals = jnp.concatenate([v_prev[base:, cols], v_ref[: base + rows, cols]], axis=0)
            dims = (((1,), (1,)), ((), ()))
            score_w = lax.dot_general(q, keys, dims, preferred_element_type=jnp.float32)
            score_v = lax.dot_general(q, vert_k[g], dims, preferred_element_type=jnp.float32)
            mask_w = in_bands(lag, g) & (window_col >= before)
            vert_lag = vert_row + (c * tok + base) - vert_pos[g]
            mask_v = (vert_lag >= 0) & ~in_bands(vert_lag, g)
            score_w = jnp.where(mask_w[None], score_w.reshape(group, rows, span), NEG)
            score_v = jnp.where(mask_v[None], score_v.reshape(group, rows, slots * BLK), NEG)
            top = jnp.maximum(
                jnp.max(score_w, axis=-1, keepdims=True), jnp.max(score_v, axis=-1, keepdims=True)
            )
            exp_w = jnp.exp2((score_w - top) * factor)
            exp_v = jnp.exp2((score_v - top) * factor)
            total = jnp.sum(exp_w, axis=-1, keepdims=True) + jnp.sum(exp_v, axis=-1, keepdims=True)
            blended = jnp.dot(
                exp_w.astype(jnp.bfloat16).reshape(group * rows, span),
                vals,
                preferred_element_type=jnp.float32,
            ) + jnp.dot(
                exp_v.astype(jnp.bfloat16).reshape(group * rows, slots * BLK),
                vert_v[g],
                preferred_element_type=jnp.float32,
            )
            result = (blended.reshape(group, rows, hd) / total).astype(jnp.bfloat16)
            for h in range(group):
                obuf[base : base + rows, (g * group + h) * hd : (g * group + h + 1) * hd] = result[h]

            @pl.when(tile != me)
            def _():
                out_copy(tile, g).start()

            @pl.when(tile == me)
            def _():
                out_own(tile, g).start()

    each(n_z - 1, lambda i: column_copy(i).wait_send())
    each(n_z, lambda i: relay_copy(i).wait_send())

    @pl.when(c < n_ctx - 1)
    def _():
        for chunk in range(n_kvh):
            for which in range(2):
                kv_copy(which, chunk).wait_send()

    for peer in range(n_kvh):
        for g in range(heads):

            @pl.when(peer != me)
            def _():
                out_copy(peer, g).wait_send()
                out_arrival(peer, g).wait_recv()

            @pl.when(peer == me)
            def _():
                out_own(peer, g).wait()


def per_device(n_ctx, n_kvh, queries, keys, values, vertical, offsets):
    tok = queries.shape[0]
    heads = vertical.shape[0]
    hd = keys.shape[1] // heads
    rows = tok // n_kvh
    hbm = pl.BlockSpec(memory_space=pltpu.HBM)
    dma = pltpu.SemaphoreType.DMA
    return pl.pallas_call(
        functools.partial(kernel, n_ctx, n_kvh),
        out_shape=jax.ShapeDtypeStruct((rows, queries.shape[1] * n_kvh), jnp.bfloat16),
        in_specs=[hbm] * 5,
        out_specs=pl.BlockSpec(memory_space=pltpu.VMEM),
        scratch_shapes=[
            pltpu.SMEM(vertical.shape, jnp.int32),
            pltpu.SMEM(offsets.shape, jnp.int32),
            pltpu.VMEM(queries.shape, jnp.bfloat16),
            pltpu.VMEM(keys.shape, jnp.bfloat16),
            pltpu.VMEM(values.shape, jnp.bfloat16),
            pltpu.VMEM(keys.shape, jnp.bfloat16),
            pltpu.VMEM(values.shape, jnp.bfloat16),
            pltpu.VMEM((n_ctx, heads, 2, BLK, hd), jnp.bfloat16),
            pltpu.VMEM(queries.shape, jnp.bfloat16),
            dma((2, n_kvh)),
            dma((2, n_kvh)),
            dma((n_ctx // 2,)),
            dma((n_ctx // 2,)),
            dma((n_ctx // 2,)),
            dma((n_ctx // 2,)),
            dma((n_kvh, heads)),
            dma((n_kvh, heads)),
            dma((heads,)),
            dma((5,)),
        ],
        compiler_params=pltpu.CompilerParams(
            collective_id=0, has_side_effects=True, vmem_limit_bytes=64 * 1024 * 1024
        ),
    )(vertical, offsets, queries, keys, values)


def solution(mesh):
    placed = (P("ctx", "kvh"), P("ctx", "kvh"), P("ctx", "kvh"), P("kvh", None), P("kvh", None))
    return jax.shard_map(
        functools.partial(per_device, mesh.shape["ctx"], mesh.shape["kvh"]),
        mesh=mesh,
        in_specs=placed,
        out_specs=P(("ctx", "kvh"), None),
        check_vma=False,
    )
```

```python
import functools
import math

import jax
import jax.numpy as jnp
from jax import lax
from jax.experimental import pallas as pl
from jax.experimental.pallas import tpu as pltpu
from jax.sharding import PartitionSpec as P

BLK = 64
NEG = -1e30
MESH = pl.DeviceIdType.MESH


def each(count, body):
    if count <= 16:
        for i in range(count):
            body(i)
    else:
        lax.fori_loop(0, count, lambda i, carry: (body(i), carry)[1], 0)


def kernel(
    n_ctx,
    n_kvh,
    vert_hbm,
    offs_hbm,
    q_hbm,
    k_hbm,
    v_hbm,
    out_ref,
    vert_ref,
    offs_ref,
    q_ref,
    k_ref,
    v_ref,
    k_prev,
    v_prev,
    gath,
    obuf,
    kv_send,
    kv_recv,
    vert_send,
    vert_recv,
    out_send,
    out_recv,
    out_local,
    load_sem,
    band_bias,
):
    c = lax.axis_index("ctx")
    me = lax.axis_index("kvh")
    tok = q_ref.shape[0]
    heads = vert_ref.shape[0]
    slots = vert_ref.shape[1]
    bands = offs_ref.shape[1]
    hd = k_ref.shape[1] // heads
    group = q_ref.shape[1] // k_ref.shape[1]
    gcols = group * hd
    rows = tok // n_kvh
    span = rows + tok
    per_shard = tok // BLK

    def ctx_peer(i):
        return lax.rem(c + 1 + i, n_ctx)

    loads = [
        pltpu.make_async_copy(src, dst, load_sem.at[i])
        for i, (src, dst) in enumerate(
            (
                (vert_hbm, vert_ref),
                (offs_hbm, offs_ref),
                (k_hbm, k_ref),
                (v_hbm, v_ref),
                (q_hbm, q_ref),
            )
        )
    ]
    for load in loads:
        load.start()

    barrier = pltpu.get_barrier_semaphore()
    each(
        n_ctx - 1,
        lambda i: pl.semaphore_signal(
            barrier, inc=1, device_id={"ctx": ctx_peer(i)}, device_id_type=MESH
        ),
    )
    for i in range(n_kvh - 1):
        pl.semaphore_signal(
            barrier,
            inc=1,
            device_id={"kvh": lax.rem(me + 1 + i, n_kvh)},
            device_id_type=MESH,
        )

    for load in loads[:4]:
        load.wait()

    for g in range(heads):
        row = jnp.int32(0)
        for j in range(slots):
            block = vert_ref[g, j]
            away = lax.div(block, per_shard) - c
            row = row + lax.rem(block, per_shard) * (1 - jnp.minimum(away * away, 1))
        row = row * BLK
        cols = slice(g * hd, (g + 1) * hd)
        gath[c, g, 0] = k_ref[pl.ds(row, BLK), cols]
        gath[c, g, 1] = v_ref[pl.ds(row, BLK), cols]

    pl.semaphore_wait(barrier, n_ctx - 1 + n_kvh - 1)

    def vert_copy(i):
        peer = ctx_peer(i)
        return pltpu.make_async_remote_copy(
            src_ref=gath.at[c],
            dst_ref=gath.at[c],
            send_sem=vert_send.at[peer],
            recv_sem=vert_recv.at[c],
            device_id={"ctx": peer},
            device_id_type=MESH,
        )

    def vert_arrival(i):
        peer = ctx_peer(i)
        return pltpu.make_async_remote_copy(
            src_ref=gath.at[peer],
            dst_ref=gath.at[peer],
            send_sem=vert_send.at[peer],
            recv_sem=vert_recv.at[peer],
            device_id={"ctx": peer},
            device_id_type=MESH,
        )

    def kv_copy(which, chunk):
        src, dst = ((k_hbm, k_prev), (v_hbm, v_prev))[which]
        part = pl.ds(chunk * rows, rows)
        return pltpu.make_async_remote_copy(
            src_ref=src.at[part],
            dst_ref=dst.at[part],
            send_sem=kv_send.at[which, chunk],
            recv_sem=kv_recv.at[which, chunk],
            device_id={"ctx": lax.rem(c + 1, n_ctx)},
            device_id_type=MESH,
        )

    each(n_ctx - 1, lambda i: vert_copy(i).start())

    @pl.when(c < n_ctx - 1)
    def _():
        for chunk in reversed(range(n_kvh)):
            for which in range(2):
                kv_copy(which, chunk).start()

    @pl.when(c == 0)
    def _():
        k_prev[...] = jnp.zeros_like(k_prev)
        v_prev[...] = jnp.zeros_like(v_prev)

    lag = (
        lax.broadcasted_iota(jnp.int32, (rows, span), 0)
        + tok
        - lax.broadcasted_iota(jnp.int32, (rows, span), 1)
    )
    window_col = lax.broadcasted_iota(jnp.int32, (rows, span), 1)
    vert_lane = lax.broadcasted_iota(jnp.int32, (1, slots * BLK), 1)
    vert_row = lax.broadcasted_iota(jnp.int32, (rows, slots * BLK), 0)

    def in_bands(distance, g):
        found = None
        for s in range(bands):
            gap = distance - offs_ref[g, s]
            hit = (gap >= 0) & (gap < BLK)
            found = hit if found is None else found | hit
        return found

    for g in range(heads):
        band_bias[g] = jnp.where(in_bands(lag, g), 0.0, NEG)
    loads[4].wait()

    each(n_ctx - 1, lambda i: vert_arrival(i).wait_recv())

    vert_k, vert_v, vert_pos = [], [], []
    for g in range(heads):
        owners = [lax.div(vert_ref[g, j], per_shard) for j in range(slots)]
        vert_k.append(jnp.concatenate([gath[o, g, 0] for o in owners], axis=0))
        vert_v.append(jnp.concatenate([gath[o, g, 1] for o in owners], axis=0))
        first = jnp.zeros_like(vert_lane)
        for j in range(slots):
            first = jnp.where(vert_lane // BLK == j, vert_ref[g, j], first)
        vert_pos.append(first * BLK + vert_lane % BLK)

    factor = math.log2(math.e) * hd**-0.5

    def out_copy(tile, g):
        return pltpu.make_async_remote_copy(
            src_ref=obuf.at[pl.ds(tile * rows, rows), pl.ds(g * gcols, gcols)],
            dst_ref=out_ref.at[
                :, pl.ds(pl.multiple_of(me * heads * gcols + g * gcols, gcols), gcols)
            ],
            send_sem=out_send.at[tile, g],
            recv_sem=out_recv.at[me, g],
            device_id={"kvh": tile},
            device_id_type=MESH,
        )

    def out_own(tile, g):
        return pltpu.make_async_copy(
            obuf.at[pl.ds(tile * rows, rows), pl.ds(g * gcols, gcols)],
            out_ref.at[
                :, pl.ds(pl.multiple_of(me * heads * gcols + g * gcols, gcols), gcols)
            ],
            out_local.at[g],
        )

    def out_arrival(peer, g):
        return pltpu.make_async_remote_copy(
            src_ref=obuf.at[pl.ds(0, rows), pl.ds(g * gcols, gcols)],
            dst_ref=out_ref.at[:, pl.ds(peer * heads * gcols + g * gcols, gcols)],
            send_sem=out_send.at[peer, g],
            recv_sem=out_recv.at[peer, g],
            device_id={"kvh": peer},
            device_id_type=MESH,
        )

    for tile in reversed(range(n_kvh)):
        base = tile * rows

        @pl.when(c > 0)
        def _():
            for which in range(2):
                kv_copy(which, tile).wait_recv()

        before = jnp.where(c == 0, tok - base, 0)
        for g in range(heads):
            cols = slice(g * hd, (g + 1) * hd)
            q = jnp.concatenate(
                [
                    q_ref[base : base + rows, (g * group + h) * hd : (g * group + h + 1) * hd]
                    for h in range(group)
                ],
                axis=0,
            )
            keys = jnp.concatenate([k_prev[base:, cols], k_ref[: base + rows, cols]], axis=0)
            vals = jnp.concatenate([v_prev[base:, cols], v_ref[: base + rows, cols]], axis=0)
            dims = (((1,), (1,)), ((), ()))
            score_w = lax.dot_general(q, keys, dims, preferred_element_type=jnp.float32)
            score_v = lax.dot_general(q, vert_k[g], dims, preferred_element_type=jnp.float32)
            bias_w = jnp.where(window_col >= before, band_bias[g], NEG)
            vert_lag = vert_row + (c * tok + base) - vert_pos[g]
            mask_v = (vert_lag >= 0) & ~in_bands(vert_lag, g)
            score_w = score_w.reshape(group, rows, span) + bias_w[None]
            score_v = jnp.where(mask_v[None], score_v.reshape(group, rows, slots * BLK), NEG)
            top = jnp.maximum(
                jnp.max(score_w, axis=-1, keepdims=True), jnp.max(score_v, axis=-1, keepdims=True)
            )
            exp_w = jnp.exp2((score_w - top) * factor)
            exp_v = jnp.exp2((score_v - top) * factor)
            total = jnp.sum(exp_w, axis=-1, keepdims=True) + jnp.sum(exp_v, axis=-1, keepdims=True)
            blended = jnp.dot(
                exp_w.astype(jnp.bfloat16).reshape(group * rows, span),
                vals,
                preferred_element_type=jnp.float32,
            ) + jnp.dot(
                exp_v.astype(jnp.bfloat16).reshape(group * rows, slots * BLK),
                vert_v[g],
                preferred_element_type=jnp.float32,
            )
            result = (blended.reshape(group, rows, hd) / total).astype(jnp.bfloat16)
            for h in range(group):
                obuf[base : base + rows, (g * group + h) * hd : (g * group + h + 1) * hd] = result[h]

            @pl.when(tile != me)
            def _():
                out_copy(tile, g).start()

            @pl.when(tile == me)
            def _():
                out_own(tile, g).start()

    each(n_ctx - 1, lambda i: vert_copy(i).wait_send())

    @pl.when(c < n_ctx - 1)
    def _():
        for chunk in range(n_kvh):
            for which in range(2):
                kv_copy(which, chunk).wait_send()

    for peer in range(n_kvh):
        for g in range(heads):

            @pl.when(peer != me)
            def _():
                out_copy(peer, g).wait_send()
                out_arrival(peer, g).wait_recv()

            @pl.when(peer == me)
            def _():
                out_own(peer, g).wait()


def per_device(n_ctx, n_kvh, queries, keys, values, vertical, offsets):
    tok = queries.shape[0]
    heads = vertical.shape[0]
    hd = keys.shape[1] // heads
    rows = tok // n_kvh
    hbm = pl.BlockSpec(memory_space=pltpu.HBM)
    dma = pltpu.SemaphoreType.DMA
    return pl.pallas_call(
        functools.partial(kernel, n_ctx, n_kvh),
        out_shape=jax.ShapeDtypeStruct((rows, queries.shape[1] * n_kvh), jnp.bfloat16),
        in_specs=[hbm] * 5,
        out_specs=pl.BlockSpec(memory_space=pltpu.VMEM),
        scratch_shapes=[
            pltpu.SMEM(vertical.shape, jnp.int32),
            pltpu.SMEM(offsets.shape, jnp.int32),
            pltpu.VMEM(queries.shape, jnp.bfloat16),
            pltpu.VMEM(keys.shape, jnp.bfloat16),
            pltpu.VMEM(values.shape, jnp.bfloat16),
            pltpu.VMEM(keys.shape, jnp.bfloat16),
            pltpu.VMEM(values.shape, jnp.bfloat16),
            pltpu.VMEM((n_ctx, heads, 2, BLK, hd), jnp.bfloat16),
            pltpu.VMEM(queries.shape, jnp.bfloat16),
            dma((2, n_kvh)),
            dma((2, n_kvh)),
            dma((n_ctx,)),
            dma((n_ctx,)),
            dma((n_kvh, heads)),
            dma((n_kvh, heads)),
            dma((heads,)),
            dma((5,)),
            pltpu.VMEM((heads, rows, rows + tok), jnp.float32),
        ],
        compiler_params=pltpu.CompilerParams(
            collective_id=0, has_side_effects=True, vmem_limit_bytes=64 * 1024 * 1024
        ),
    )(vertical, offsets, queries, keys, values)


def solution(mesh):
    placed = (P("ctx", "kvh"), P("ctx", "kvh"), P("ctx", "kvh"), P("kvh", None), P("kvh", None))
    return jax.shard_map(
        functools.partial(per_device, mesh.shape["ctx"], mesh.shape["kvh"]),
        mesh=mesh,
        in_specs=placed,
        out_specs=P(("ctx", "kvh"), None),
        check_vma=False,
    )
```

```python
import functools
import math

import jax
import jax.numpy as jnp
from jax import lax
from jax.experimental import pallas as pl
from jax.experimental.pallas import tpu as pltpu
from jax.sharding import PartitionSpec as P

BLK = 64
NEG = -1e30
MESH = pl.DeviceIdType.MESH


def each(count, body):
    if count <= 16:
        for i in range(count):
            body(i)
    else:
        lax.fori_loop(0, count, lambda i, carry: (body(i), carry)[1], 0)


def kernel(
    n_ctx,
    n_kvh,
    vert_hbm,
    offs_hbm,
    q_hbm,
    k_hbm,
    v_hbm,
    out_ref,
    vert_ref,
    offs_ref,
    q_ref,
    k_ref,
    v_ref,
    k_prev,
    v_prev,
    gath,
    obuf,
    kv_send,
    kv_recv,
    vert_send,
    vert_recv,
    out_send,
    out_recv,
    out_local,
    load_sem,
    band_bias,
    relay,
    relay_send,
    relay_recv,
):
    c = lax.axis_index("ctx")
    me = lax.axis_index("kvh")
    tok = q_ref.shape[0]
    heads = vert_ref.shape[0]
    slots = vert_ref.shape[1]
    bands = offs_ref.shape[1]
    hd = k_ref.shape[1] // heads
    group = q_ref.shape[1] // k_ref.shape[1]
    gcols = group * hd
    rows = tok // n_kvh
    span = rows + tok
    per_shard = tok // BLK

    def ctx_peer(i):
        return lax.rem(c + 1 + i, n_ctx)

    loads = [
        pltpu.make_async_copy(src, dst, load_sem.at[i])
        for i, (src, dst) in enumerate(
            (
                (vert_hbm, vert_ref),
                (offs_hbm, offs_ref),
                (k_hbm, k_ref),
                (v_hbm, v_ref),
                (q_hbm, q_ref),
            )
        )
    ]
    for load in loads:
        load.start()

    barrier = pltpu.get_barrier_semaphore()
    each(
        n_ctx - 1,
        lambda i: pl.semaphore_signal(
            barrier, inc=1, device_id={"ctx": ctx_peer(i)}, device_id_type=MESH
        ),
    )
    for i in range(n_kvh - 1):
        pl.semaphore_signal(
            barrier,
            inc=1,
            device_id={"kvh": lax.rem(me + 1 + i, n_kvh)},
            device_id_type=MESH,
        )

    for load in loads[:4]:
        load.wait()

    for g in range(heads):
        row = jnp.int32(0)
        for j in range(slots):
            block = vert_ref[g, j]
            away = lax.div(block, per_shard) - c
            row = row + lax.rem(block, per_shard) * (1 - jnp.minimum(away * away, 1))
        row = row * BLK
        cols = slice(g * hd, (g + 1) * hd)
        gath[c, g, 0] = k_ref[pl.ds(row, BLK), cols]
        gath[c, g, 1] = v_ref[pl.ds(row, BLK), cols]

    pl.semaphore_wait(barrier, n_ctx - 1 + n_kvh - 1)

    def vert_copy(i):
        peer = ctx_peer(i)
        return pltpu.make_async_remote_copy(
            src_ref=gath.at[c],
            dst_ref=gath.at[c],
            send_sem=vert_send.at[peer],
            recv_sem=vert_recv.at[c],
            device_id={"ctx": peer},
            device_id_type=MESH,
        )

    def vert_arrival(i):
        peer = ctx_peer(i)
        return pltpu.make_async_remote_copy(
            src_ref=gath.at[peer],
            dst_ref=gath.at[peer],
            send_sem=vert_send.at[peer],
            recv_sem=vert_recv.at[peer],
            device_id={"ctx": peer},
            device_id_type=MESH,
        )

    x = c % 2
    sides = ((k_hbm, k_prev), (v_hbm, v_prev))

    def kv_copy(which, chunk):
        src, dst = sides[which]
        part = pl.ds(chunk * rows, rows)
        return pltpu.make_async_remote_copy(
            src_ref=src.at[part],
            dst_ref=dst.at[part],
            send_sem=kv_send.at[which, chunk],
            recv_sem=kv_recv.at[which, chunk],
            device_id={"ctx": lax.rem(c + 1, n_ctx)},
            device_id_type=MESH,
        )

    def odd_copy(which, chunk):
        part = pl.ds(chunk * rows, rows)
        return pltpu.make_async_remote_copy(
            src_ref=sides[which][0].at[part],
            dst_ref=relay.at[part],
            send_sem=kv_send.at[which, chunk],
            recv_sem=relay_recv.at[chunk],
            device_id={"ctx": (c - 1, c + 2)[which]},
            device_id_type=MESH,
        )

    def onward_copy(which, chunk):
        part = pl.ds(chunk * rows, rows)
        return pltpu.make_async_remote_copy(
            src_ref=relay.at[part],
            dst_ref=sides[which][1].at[part],
            send_sem=relay_send.at[chunk],
            recv_sem=kv_recv.at[which, chunk],
            device_id={"ctx": (c + 2, c - 1)[which]},
            device_id_type=MESH,
        )

    odd_sends = (x == 1) & (c < n_ctx - 1)
    relays = ((x == 0) & (c < n_ctx - 2), (x == 1) & (c > 1))

    each(n_ctx - 1, lambda i: vert_copy(i).start())
    for chunk in reversed(range(n_kvh)):
        for which in range(2):

            @pl.when(x == 0)
            def _():
                kv_copy(which, chunk).start()

            @pl.when(odd_sends)
            def _():
                odd_copy(which, chunk).start()

    @pl.when(c == 0)
    def _():
        k_prev[...] = jnp.zeros_like(k_prev)
        v_prev[...] = jnp.zeros_like(v_prev)

    lag = (
        lax.broadcasted_iota(jnp.int32, (rows, span), 0)
        + tok
        - lax.broadcasted_iota(jnp.int32, (rows, span), 1)
    )
    window_col = lax.broadcasted_iota(jnp.int32, (rows, span), 1)
    vert_lane = lax.broadcasted_iota(jnp.int32, (1, slots * BLK), 1)
    vert_row = lax.broadcasted_iota(jnp.int32, (rows, slots * BLK), 0)

    def in_bands(distance, g):
        found = None
        for s in range(bands):
            gap = distance - offs_ref[g, s]
            hit = (gap >= 0) & (gap < BLK)
            found = hit if found is None else found | hit
        return found

    for g in range(heads):
        band_bias[g] = jnp.where(in_bands(lag, g), 0.0, NEG)
    loads[4].wait()

    for which in range(2):

        @pl.when(relays[which])
        def _():
            for chunk in reversed(range(n_kvh)):
                odd_copy(which, chunk).wait_recv()
                onward_copy(which, chunk).start()

    each(n_ctx - 1, lambda i: vert_arrival(i).wait_recv())

    vert_k, vert_v, vert_pos = [], [], []
    for g in range(heads):
        owners = [lax.div(vert_ref[g, j], per_shard) for j in range(slots)]
        vert_k.append(jnp.concatenate([gath[o, g, 0] for o in owners], axis=0))
        vert_v.append(jnp.concatenate([gath[o, g, 1] for o in owners], axis=0))
        first = jnp.zeros_like(vert_lane)
        for j in range(slots):
            first = jnp.where(vert_lane // BLK == j, vert_ref[g, j], first)
        vert_pos.append(first * BLK + vert_lane % BLK)

    factor = math.log2(math.e) * hd**-0.5

    def out_copy(tile, g):
        return pltpu.make_async_remote_copy(
            src_ref=obuf.at[pl.ds(tile * rows, rows), pl.ds(g * gcols, gcols)],
            dst_ref=out_ref.at[
                :, pl.ds(pl.multiple_of(me * heads * gcols + g * gcols, gcols), gcols)
            ],
            send_sem=out_send.at[tile, g],
            recv_sem=out_recv.at[me, g],
            device_id={"kvh": tile},
            device_id_type=MESH,
        )

    def out_own(tile, g):
        return pltpu.make_async_copy(
            obuf.at[pl.ds(tile * rows, rows), pl.ds(g * gcols, gcols)],
            out_ref.at[
                :, pl.ds(pl.multiple_of(me * heads * gcols + g * gcols, gcols), gcols)
            ],
            out_local.at[g],
        )

    def out_arrival(peer, g):
        return pltpu.make_async_remote_copy(
            src_ref=obuf.at[pl.ds(0, rows), pl.ds(g * gcols, gcols)],
            dst_ref=out_ref.at[:, pl.ds(peer * heads * gcols + g * gcols, gcols)],
            send_sem=out_send.at[peer, g],
            recv_sem=out_recv.at[peer, g],
            device_id={"kvh": peer},
            device_id_type=MESH,
        )

    for tile in reversed(range(n_kvh)):
        base = tile * rows

        @pl.when(c > 0)
        def _():
            for which in range(2):
                kv_copy(which, tile).wait_recv()

        before = jnp.where(c == 0, tok - base, 0)
        for g in range(heads):
            cols = slice(g * hd, (g + 1) * hd)
            q = jnp.concatenate(
                [
                    q_ref[base : base + rows, (g * group + h) * hd : (g * group + h + 1) * hd]
                    for h in range(group)
                ],
                axis=0,
            )
            keys = jnp.concatenate([k_prev[base:, cols], k_ref[: base + rows, cols]], axis=0)
            vals = jnp.concatenate([v_prev[base:, cols], v_ref[: base + rows, cols]], axis=0)
            dims = (((1,), (1,)), ((), ()))
            score_w = lax.dot_general(q, keys, dims, preferred_element_type=jnp.float32)
            score_v = lax.dot_general(q, vert_k[g], dims, preferred_element_type=jnp.float32)
            bias_w = jnp.where(window_col >= before, band_bias[g], NEG)
            vert_lag = vert_row + (c * tok + base) - vert_pos[g]
            mask_v = (vert_lag >= 0) & ~in_bands(vert_lag, g)
            score_w = score_w.reshape(group, rows, span) + bias_w[None]
            score_v = jnp.where(mask_v[None], score_v.reshape(group, rows, slots * BLK), NEG)
            top = jnp.maximum(
                jnp.max(score_w, axis=-1, keepdims=True), jnp.max(score_v, axis=-1, keepdims=True)
            )
            exp_w = jnp.exp2((score_w - top) * factor)
            exp_v = jnp.exp2((score_v - top) * factor)
            total = jnp.sum(exp_w, axis=-1, keepdims=True) + jnp.sum(exp_v, axis=-1, keepdims=True)
            blended = jnp.dot(
                exp_w.astype(jnp.bfloat16).reshape(group * rows, span),
                vals,
                preferred_element_type=jnp.float32,
            ) + jnp.dot(
                exp_v.astype(jnp.bfloat16).reshape(group * rows, slots * BLK),
                vert_v[g],
                preferred_element_type=jnp.float32,
            )
            result = (blended.reshape(group, rows, hd) / total).astype(jnp.bfloat16)
            for h in range(group):
                obuf[base : base + rows, (g * group + h) * hd : (g * group + h + 1) * hd] = result[h]

            @pl.when(tile != me)
            def _():
                out_copy(tile, g).start()

            @pl.when(tile == me)
            def _():
                out_own(tile, g).start()

    each(n_ctx - 1, lambda i: vert_copy(i).wait_send())

    for chunk in range(n_kvh):
        for which in range(2):

            @pl.when((x == 0) | odd_sends)
            def _():
                kv_copy(which, chunk).wait_send()

            @pl.when(relays[which])
            def _():
                onward_copy(which, chunk).wait_send()

    for peer in range(n_kvh):
        for g in range(heads):

            @pl.when(peer != me)
            def _():
                out_copy(peer, g).wait_send()
                out_arrival(peer, g).wait_recv()

            @pl.when(peer == me)
            def _():
                out_own(peer, g).wait()


def per_device(n_ctx, n_kvh, queries, keys, values, vertical, offsets):
    tok = queries.shape[0]
    heads = vertical.shape[0]
    hd = keys.shape[1] // heads
    rows = tok // n_kvh
    hbm = pl.BlockSpec(memory_space=pltpu.HBM)
    dma = pltpu.SemaphoreType.DMA
    return pl.pallas_call(
        functools.partial(kernel, n_ctx, n_kvh),
        out_shape=jax.ShapeDtypeStruct((rows, queries.shape[1] * n_kvh), jnp.bfloat16),
        in_specs=[hbm] * 5,
        out_specs=pl.BlockSpec(memory_space=pltpu.VMEM),
        scratch_shapes=[
            pltpu.SMEM(vertical.shape, jnp.int32),
            pltpu.SMEM(offsets.shape, jnp.int32),
            pltpu.VMEM(queries.shape, jnp.bfloat16),
            pltpu.VMEM(keys.shape, jnp.bfloat16),
            pltpu.VMEM(values.shape, jnp.bfloat16),
            pltpu.VMEM(keys.shape, jnp.bfloat16),
            pltpu.VMEM(values.shape, jnp.bfloat16),
            pltpu.VMEM((n_ctx, heads, 2, BLK, hd), jnp.bfloat16),
            pltpu.VMEM(queries.shape, jnp.bfloat16),
            dma((2, n_kvh)),
            dma((2, n_kvh)),
            dma((n_ctx,)),
            dma((n_ctx,)),
            dma((n_kvh, heads)),
            dma((n_kvh, heads)),
            dma((heads,)),
            dma((5,)),
            pltpu.VMEM((heads, rows, rows + tok), jnp.float32),
            pltpu.VMEM(keys.shape, jnp.bfloat16),
            dma((n_kvh,)),
            dma((n_kvh,)),
        ],
        compiler_params=pltpu.CompilerParams(
            collective_id=0, has_side_effects=True, vmem_limit_bytes=64 * 1024 * 1024
        ),
    )(vertical, offsets, queries, keys, values)


def solution(mesh):
    placed = (P("ctx", "kvh"), P("ctx", "kvh"), P("ctx", "kvh"), P("kvh", None), P("kvh", None))
    return jax.shard_map(
        functools.partial(per_device, mesh.shape["ctx"], mesh.shape["kvh"]),
        mesh=mesh,
        in_specs=placed,
        out_specs=P(("ctx", "kvh"), None),
        check_vma=False,
    )
```

```python
import functools
import math

import jax
import jax.numpy as jnp
from jax import lax
from jax.experimental import pallas as pl
from jax.experimental.pallas import tpu as pltpu
from jax.sharding import PartitionSpec as P

BLK = 64
NEG = -1e30
MESH = pl.DeviceIdType.MESH


def each(count, body):
    if count <= 16:
        for i in range(count):
            body(i)
    else:
        lax.fori_loop(0, count, lambda i, carry: (body(i), carry)[1], 0)


def kernel(
    n_ctx,
    n_kvh,
    vert_hbm,
    offs_hbm,
    q_hbm,
    k_hbm,
    v_hbm,
    out_ref,
    vert_ref,
    offs_ref,
    q_ref,
    k_ref,
    v_ref,
    k_prev,
    v_prev,
    gath,
    obuf,
    kv_send,
    kv_recv,
    vert_send,
    vert_recv,
    out_send,
    out_recv,
    out_local,
    load_sem,
    band_bias,
    win_top,
    win_total,
    win_out,
):
    c = lax.axis_index("ctx")
    me = lax.axis_index("kvh")
    tok = q_ref.shape[0]
    heads = vert_ref.shape[0]
    slots = vert_ref.shape[1]
    bands = offs_ref.shape[1]
    hd = k_ref.shape[1] // heads
    group = q_ref.shape[1] // k_ref.shape[1]
    gcols = group * hd
    rows = tok // n_kvh
    span = rows + tok
    per_shard = tok // BLK

    def ctx_peer(i):
        return lax.rem(c + 1 + i, n_ctx)

    loads = [
        pltpu.make_async_copy(src, dst, load_sem.at[i])
        for i, (src, dst) in enumerate(
            (
                (vert_hbm, vert_ref),
                (offs_hbm, offs_ref),
                (k_hbm, k_ref),
                (v_hbm, v_ref),
                (q_hbm, q_ref),
            )
        )
    ]
    for load in loads:
        load.start()

    barrier = pltpu.get_barrier_semaphore()
    each(
        n_ctx - 1,
        lambda i: pl.semaphore_signal(
            barrier, inc=1, device_id={"ctx": ctx_peer(i)}, device_id_type=MESH
        ),
    )
    for i in range(n_kvh - 1):
        pl.semaphore_signal(
            barrier,
            inc=1,
            device_id={"kvh": lax.rem(me + 1 + i, n_kvh)},
            device_id_type=MESH,
        )

    for load in loads[:4]:
        load.wait()

    for g in range(heads):
        row = jnp.int32(0)
        for j in range(slots):
            block = vert_ref[g, j]
            away = lax.div(block, per_shard) - c
            row = row + lax.rem(block, per_shard) * (1 - jnp.minimum(away * away, 1))
        row = row * BLK
        cols = slice(g * hd, (g + 1) * hd)
        gath[c, g, 0] = k_ref[pl.ds(row, BLK), cols]
        gath[c, g, 1] = v_ref[pl.ds(row, BLK), cols]

    pl.semaphore_wait(barrier, n_ctx - 1 + n_kvh - 1)

    def vert_copy(i):
        peer = ctx_peer(i)
        return pltpu.make_async_remote_copy(
            src_ref=gath.at[c],
            dst_ref=gath.at[c],
            send_sem=vert_send.at[peer],
            recv_sem=vert_recv.at[c],
            device_id={"ctx": peer},
            device_id_type=MESH,
        )

    def vert_arrival(i):
        peer = ctx_peer(i)
        return pltpu.make_async_remote_copy(
            src_ref=gath.at[peer],
            dst_ref=gath.at[peer],
            send_sem=vert_send.at[peer],
            recv_sem=vert_recv.at[peer],
            device_id={"ctx": peer},
            device_id_type=MESH,
        )

    def kv_copy(which, chunk):
        src, dst = ((k_hbm, k_prev), (v_hbm, v_prev))[which]
        part = pl.ds(chunk * rows, rows)
        return pltpu.make_async_remote_copy(
            src_ref=src.at[part],
            dst_ref=dst.at[part],
            send_sem=kv_send.at[which, chunk],
            recv_sem=kv_recv.at[which, chunk],
            device_id={"ctx": lax.rem(c + 1, n_ctx)},
            device_id_type=MESH,
        )

    @pl.when(c < n_ctx - 1)
    def _():
        for chunk in reversed(range(n_kvh)):
            for which in range(2):
                kv_copy(which, chunk).start()

    each(n_ctx - 1, lambda i: vert_copy(i).start())

    @pl.when(c == 0)
    def _():
        k_prev[...] = jnp.zeros_like(k_prev)
        v_prev[...] = jnp.zeros_like(v_prev)

    lag = (
        lax.broadcasted_iota(jnp.int32, (rows, span), 0)
        + tok
        - lax.broadcasted_iota(jnp.int32, (rows, span), 1)
    )
    window_col = lax.broadcasted_iota(jnp.int32, (rows, span), 1)
    vert_lane = lax.broadcasted_iota(jnp.int32, (1, slots * BLK), 1)
    vert_row = lax.broadcasted_iota(jnp.int32, (rows, slots * BLK), 0)

    def in_bands(distance, g):
        found = None
        for s in range(bands):
            gap = distance - offs_ref[g, s]
            hit = (gap >= 0) & (gap < BLK)
            found = hit if found is None else found | hit
        return found

    for g in range(heads):
        band_bias[g] = jnp.where(in_bands(lag, g), 0.0, NEG)
    loads[4].wait()

    factor = math.log2(math.e) * hd**-0.5

    def out_copy(tile, g):
        return pltpu.make_async_remote_copy(
            src_ref=obuf.at[pl.ds(tile * rows, rows), pl.ds(g * gcols, gcols)],
            dst_ref=out_ref.at[
                :, pl.ds(pl.multiple_of(me * heads * gcols + g * gcols, gcols), gcols)
            ],
            send_sem=out_send.at[tile, g],
            recv_sem=out_recv.at[me, g],
            device_id={"kvh": tile},
            device_id_type=MESH,
        )

    def out_own(tile, g):
        return pltpu.make_async_copy(
            obuf.at[pl.ds(tile * rows, rows), pl.ds(g * gcols, gcols)],
            out_ref.at[
                :, pl.ds(pl.multiple_of(me * heads * gcols + g * gcols, gcols), gcols)
            ],
            out_local.at[g],
        )

    def out_arrival(peer, g):
        return pltpu.make_async_remote_copy(
            src_ref=obuf.at[pl.ds(0, rows), pl.ds(g * gcols, gcols)],
            dst_ref=out_ref.at[:, pl.ds(peer * heads * gcols + g * gcols, gcols)],
            send_sem=out_send.at[peer, g],
            recv_sem=out_recv.at[peer, g],
            device_id={"kvh": peer},
            device_id_type=MESH,
        )

    dims = (((1,), (1,)), ((), ()))

    for tile in reversed(range(n_kvh)):
        base = tile * rows

        @pl.when(c > 0)
        def _():
            for which in range(2):
                kv_copy(which, tile).wait_recv()

        before = jnp.where(c == 0, tok - base, 0)
        for g in range(heads):
            cols = slice(g * hd, (g + 1) * hd)
            q = jnp.concatenate(
                [
                    q_ref[base : base + rows, (g * group + h) * hd : (g * group + h + 1) * hd]
                    for h in range(group)
                ],
                axis=0,
            )
            keys = jnp.concatenate([k_prev[base:, cols], k_ref[: base + rows, cols]], axis=0)
            vals = jnp.concatenate([v_prev[base:, cols], v_ref[: base + rows, cols]], axis=0)
            score = lax.dot_general(q, keys, dims, preferred_element_type=jnp.float32)
            bias = jnp.where(window_col >= before, band_bias[g], NEG)
            score = score.reshape(group, rows, span) + bias[None]
            top = jnp.max(score, axis=-1, keepdims=True)
            weight = jnp.exp2((score - top) * factor)
            win_top[tile, g] = top.reshape(group * rows, 1)
            win_total[tile, g] = jnp.sum(weight, axis=-1, keepdims=True).reshape(group * rows, 1)
            win_out[tile, g] = jnp.dot(
                weight.astype(jnp.bfloat16).reshape(group * rows, span),
                vals,
                preferred_element_type=jnp.float32,
            )

    each(n_ctx - 1, lambda i: vert_arrival(i).wait_recv())

    vert_k, vert_v, vert_pos = [], [], []
    for g in range(heads):
        owners = [lax.div(vert_ref[g, j], per_shard) for j in range(slots)]
        vert_k.append(jnp.concatenate([gath[o, g, 0] for o in owners], axis=0))
        vert_v.append(jnp.concatenate([gath[o, g, 1] for o in owners], axis=0))
        first = jnp.zeros_like(vert_lane)
        for j in range(slots):
            first = jnp.where(vert_lane // BLK == j, vert_ref[g, j], first)
        vert_pos.append(first * BLK + vert_lane % BLK)

    half = n_kvh // 2
    for turn in range(n_kvh):
        tile = lax.rem(half * (1 - me // half) + turn, n_kvh)
        base = pl.multiple_of(tile * rows, rows)
        for g in range(heads):
            q = jnp.concatenate(
                [
                    q_ref[pl.ds(base, rows), (g * group + h) * hd : (g * group + h + 1) * hd]
                    for h in range(group)
                ],
                axis=0,
            )
            score = lax.dot_general(q, vert_k[g], dims, preferred_element_type=jnp.float32)
            vert_lag = vert_row + (c * tok + base) - vert_pos[g]
            mask = (vert_lag >= 0) & ~in_bands(vert_lag, g)
            score = jnp.where(mask[None], score.reshape(group, rows, slots * BLK), NEG)
            score = score.reshape(group * rows, slots * BLK)
            before_top = win_top[tile, g]
            top = jnp.maximum(before_top, jnp.max(score, axis=-1, keepdims=True))
            weight = jnp.exp2((score - top) * factor)
            fade = jnp.exp2((before_top - top) * factor)
            total = win_total[tile, g] * fade + jnp.sum(weight, axis=-1, keepdims=True)
            blended = win_out[tile, g] * fade + jnp.dot(
                weight.astype(jnp.bfloat16), vert_v[g], preferred_element_type=jnp.float32
            )
            result = (blended / total).astype(jnp.bfloat16)
            for h in range(group):
                obuf[pl.ds(base, rows), (g * group + h) * hd : (g * group + h + 1) * hd] = result[
                    h * rows : (h + 1) * rows
                ]

            @pl.when(tile != me)
            def _():
                out_copy(tile, g).start()

            @pl.when(tile == me)
            def _():
                out_own(tile, g).start()

    each(n_ctx - 1, lambda i: vert_copy(i).wait_send())

    @pl.when(c < n_ctx - 1)
    def _():
        for chunk in range(n_kvh):
            for which in range(2):
                kv_copy(which, chunk).wait_send()

    for peer in range(n_kvh):
        for g in range(heads):

            @pl.when(peer != me)
            def _():
                out_copy(peer, g).wait_send()
                out_arrival(peer, g).wait_recv()

            @pl.when(peer == me)
            def _():
                out_own(peer, g).wait()


def per_device(n_ctx, n_kvh, queries, keys, values, vertical, offsets):
    tok = queries.shape[0]
    heads = vertical.shape[0]
    hd = keys.shape[1] // heads
    rows = tok // n_kvh
    group = queries.shape[1] // keys.shape[1]
    hbm = pl.BlockSpec(memory_space=pltpu.HBM)
    dma = pltpu.SemaphoreType.DMA
    return pl.pallas_call(
        functools.partial(kernel, n_ctx, n_kvh),
        out_shape=jax.ShapeDtypeStruct((rows, queries.shape[1] * n_kvh), jnp.bfloat16),
        in_specs=[hbm] * 5,
        out_specs=pl.BlockSpec(memory_space=pltpu.VMEM),
        scratch_shapes=[
            pltpu.SMEM(vertical.shape, jnp.int32),
            pltpu.SMEM(offsets.shape, jnp.int32),
            pltpu.VMEM(queries.shape, jnp.bfloat16),
            pltpu.VMEM(keys.shape, jnp.bfloat16),
            pltpu.VMEM(values.shape, jnp.bfloat16),
            pltpu.VMEM(keys.shape, jnp.bfloat16),
            pltpu.VMEM(values.shape, jnp.bfloat16),
            pltpu.VMEM((n_ctx, heads, 2, BLK, hd), jnp.bfloat16),
            pltpu.VMEM(queries.shape, jnp.bfloat16),
            dma((2, n_kvh)),
            dma((2, n_kvh)),
            dma((n_ctx,)),
            dma((n_ctx,)),
            dma((n_kvh, heads)),
            dma((n_kvh, heads)),
            dma((heads,)),
            dma((5,)),
            pltpu.VMEM((heads, rows, rows + tok), jnp.float32),
            pltpu.VMEM((n_kvh, heads, group * rows, 1), jnp.float32),
            pltpu.VMEM((n_kvh, heads, group * rows, 1), jnp.float32),
            pltpu.VMEM((n_kvh, heads, group * rows, hd), jnp.float32),
        ],
        compiler_params=pltpu.CompilerParams(
            collective_id=0, has_side_effects=True, vmem_limit_bytes=64 * 1024 * 1024
        ),
    )(vertical, offsets, queries, keys, values)


def solution(mesh):
    placed = (P("ctx", "kvh"), P("ctx", "kvh"), P("ctx", "kvh"), P("kvh", None), P("kvh", None))
    return jax.shard_map(
        functools.partial(per_device, mesh.shape["ctx"], mesh.shape["kvh"]),
        mesh=mesh,
        in_specs=placed,
        out_specs=P(("ctx", "kvh"), None),
        check_vma=False,
    )
```

```python
import functools
import math

import jax
import jax.numpy as jnp
from jax import lax
from jax.experimental import pallas as pl
from jax.experimental.pallas import tpu as pltpu
from jax.sharding import PartitionSpec as P

BLK = 64
NEG = -1e30
MESH = pl.DeviceIdType.MESH


def each(count, body):
    if count <= 16:
        for i in range(count):
            body(i)
    else:
        lax.fori_loop(0, count, lambda i, carry: (body(i), carry)[1], 0)


def kernel(
    n_ctx,
    n_kvh,
    vert_hbm,
    offs_hbm,
    q_hbm,
    k_hbm,
    v_hbm,
    out_ref,
    vert_ref,
    offs_ref,
    q_ref,
    k_ref,
    v_ref,
    k_prev,
    v_prev,
    gath,
    obuf,
    kv_send,
    kv_recv,
    col_send,
    col_recv,
    vrelay_send,
    vrelay_recv,
    out_send,
    out_recv,
    out_local,
    load_sem,
    band_bias,
    win_top,
    win_total,
    win_out,
    relay,
    relay_send,
    relay_recv,
):
    c = lax.axis_index("ctx")
    me = lax.axis_index("kvh")
    tok = q_ref.shape[0]
    heads = vert_ref.shape[0]
    slots = vert_ref.shape[1]
    bands = offs_ref.shape[1]
    hd = k_ref.shape[1] // heads
    group = q_ref.shape[1] // k_ref.shape[1]
    gcols = group * hd
    rows = tok // n_kvh
    span = rows + tok
    per_shard = tok // BLK

    z, x = c // 2, c % 2
    n_z = n_ctx // 2
    partner = c + 1 - 2 * x

    def column(i):
        return lax.rem(z + 1 + i, n_z)

    def ctx_peer(i):
        return lax.rem(c + 1 + i, n_ctx)

    loads = [
        pltpu.make_async_copy(src, dst, load_sem.at[i])
        for i, (src, dst) in enumerate(
            (
                (vert_hbm, vert_ref),
                (offs_hbm, offs_ref),
                (k_hbm, k_ref),
                (v_hbm, v_ref),
                (q_hbm, q_ref),
            )
        )
    ]
    for load in loads:
        load.start()

    barrier = pltpu.get_barrier_semaphore()
    each(
        n_ctx - 1,
        lambda i: pl.semaphore_signal(
            barrier, inc=1, device_id={"ctx": ctx_peer(i)}, device_id_type=MESH
        ),
    )
    for i in range(n_kvh - 1):
        pl.semaphore_signal(
            barrier,
            inc=1,
            device_id={"kvh": lax.rem(me + 1 + i, n_kvh)},
            device_id_type=MESH,
        )

    for load in loads[:4]:
        load.wait()

    for g in range(heads):
        row = jnp.int32(0)
        for j in range(slots):
            block = vert_ref[g, j]
            away = lax.div(block, per_shard) - c
            row = row + lax.rem(block, per_shard) * (1 - jnp.minimum(away * away, 1))
        row = row * BLK
        cols = slice(g * hd, (g + 1) * hd)
        gath[c, g, 0] = k_ref[pl.ds(row, BLK), cols]
        gath[c, g, 1] = v_ref[pl.ds(row, BLK), cols]

    pl.semaphore_wait(barrier, n_ctx - 1 + n_kvh - 1)

    def column_copy(i):
        peer = column(i)
        return pltpu.make_async_remote_copy(
            src_ref=gath.at[c],
            dst_ref=gath.at[c],
            send_sem=col_send.at[peer],
            recv_sem=col_recv.at[z],
            device_id={"ctx": 2 * peer + x},
            device_id_type=MESH,
        )

    def column_arrival(i):
        peer = column(i)
        return pltpu.make_async_remote_copy(
            src_ref=gath.at[2 * peer + x],
            dst_ref=gath.at[2 * peer + x],
            send_sem=col_send.at[peer],
            recv_sem=col_recv.at[peer],
            device_id={"ctx": 2 * peer + x},
            device_id_type=MESH,
        )

    def relay_copy(row):
        part = gath.at[2 * row + x]
        return pltpu.make_async_remote_copy(
            src_ref=part,
            dst_ref=part,
            send_sem=vrelay_send.at[row],
            recv_sem=vrelay_recv.at[row],
            device_id={"ctx": partner},
            device_id_type=MESH,
        )

    def relay_arrival(row):
        part = gath.at[2 * row + 1 - x]
        return pltpu.make_async_remote_copy(
            src_ref=part,
            dst_ref=part,
            send_sem=vrelay_send.at[row],
            recv_sem=vrelay_recv.at[row],
            device_id={"ctx": partner},
            device_id_type=MESH,
        )

    def relay_round(i):
        column_arrival(i).wait_recv()
        relay_copy(column(i)).start()

    sides = ((k_hbm, k_prev), (v_hbm, v_prev))

    def kv_copy(which, chunk):
        src, dst = sides[which]
        part = pl.ds(chunk * rows, rows)
        return pltpu.make_async_remote_copy(
            src_ref=src.at[part],
            dst_ref=dst.at[part],
            send_sem=kv_send.at[which, chunk],
            recv_sem=kv_recv.at[which, chunk],
            device_id={"ctx": lax.rem(c + 1, n_ctx)},
            device_id_type=MESH,
        )

    def odd_copy(which, chunk):
        part = pl.ds(chunk * rows, rows)
        return pltpu.make_async_remote_copy(
            src_ref=sides[which][0].at[part],
            dst_ref=relay.at[part],
            send_sem=kv_send.at[which, chunk],
            recv_sem=relay_recv.at[chunk],
            device_id={"ctx": (c - 1, c + 2)[which]},
            device_id_type=MESH,
        )

    def onward_copy(which, chunk):
        part = pl.ds(chunk * rows, rows)
        return pltpu.make_async_remote_copy(
            src_ref=relay.at[part],
            dst_ref=sides[which][1].at[part],
            send_sem=relay_send.at[chunk],
            recv_sem=kv_recv.at[which, chunk],
            device_id={"ctx": (c + 2, c - 1)[which]},
            device_id_type=MESH,
        )

    odd_sends = (x == 1) & (c < n_ctx - 1)
    relays = ((x == 0) & (c < n_ctx - 2), (x == 1) & (c > 1))

    each(n_z - 1, lambda i: column_copy(i).start())
    relay_copy(z).start()
    for chunk in reversed(range(n_kvh)):
        for which in range(2):

            @pl.when(x == 0)
            def _():
                kv_copy(which, chunk).start()

            @pl.when(odd_sends)
            def _():
                odd_copy(which, chunk).start()

    @pl.when(c == 0)
    def _():
        k_prev[...] = jnp.zeros_like(k_prev)
        v_prev[...] = jnp.zeros_like(v_prev)

    lag = (
        lax.broadcasted_iota(jnp.int32, (rows, span), 0)
        + tok
        - lax.broadcasted_iota(jnp.int32, (rows, span), 1)
    )
    window_col = lax.broadcasted_iota(jnp.int32, (rows, span), 1)
    vert_lane = lax.broadcasted_iota(jnp.int32, (1, slots * BLK), 1)
    vert_row = lax.broadcasted_iota(jnp.int32, (rows, slots * BLK), 0)

    def in_bands(distance, g):
        found = None
        for s in range(bands):
            gap = distance - offs_ref[g, s]
            hit = (gap >= 0) & (gap < BLK)
            found = hit if found is None else found | hit
        return found

    for g in range(heads):
        band_bias[g] = jnp.where(in_bands(lag, g), 0.0, NEG)
    loads[4].wait()

    factor = math.log2(math.e) * hd**-0.5

    def out_copy(tile, g):
        return pltpu.make_async_remote_copy(
            src_ref=obuf.at[pl.ds(tile * rows, rows), pl.ds(g * gcols, gcols)],
            dst_ref=out_ref.at[
                :, pl.ds(pl.multiple_of(me * heads * gcols + g * gcols, gcols), gcols)
            ],
            send_sem=out_send.at[tile, g],
            recv_sem=out_recv.at[me, g],
            device_id={"kvh": tile},
            device_id_type=MESH,
        )

    def out_own(tile, g):
        return pltpu.make_async_copy(
            obuf.at[pl.ds(tile * rows, rows), pl.ds(g * gcols, gcols)],
            out_ref.at[
                :, pl.ds(pl.multiple_of(me * heads * gcols + g * gcols, gcols), gcols)
            ],
            out_local.at[g],
        )

    def out_arrival(peer, g):
        return pltpu.make_async_remote_copy(
            src_ref=obuf.at[pl.ds(0, rows), pl.ds(g * gcols, gcols)],
            dst_ref=out_ref.at[:, pl.ds(peer * heads * gcols + g * gcols, gcols)],
            send_sem=out_send.at[peer, g],
            recv_sem=out_recv.at[peer, g],
            device_id={"kvh": peer},
            device_id_type=MESH,
        )

    dims = (((1,), (1,)), ((), ()))

    for tile in reversed(range(n_kvh)):
        base = tile * rows
        for which in range(2):

            @pl.when(relays[which])
            def _():
                odd_copy(which, tile).wait_recv()
                onward_copy(which, tile).start()

        if tile == n_kvh - 2:
            each(n_z - 1, relay_round)

        @pl.when(c > 0)
        def _():
            for which in range(2):
                kv_copy(which, tile).wait_recv()

        before = jnp.where(c == 0, tok - base, 0)
        for g in range(heads):
            cols = slice(g * hd, (g + 1) * hd)
            q = jnp.concatenate(
                [
                    q_ref[base : base + rows, (g * group + h) * hd : (g * group + h + 1) * hd]
                    for h in range(group)
                ],
                axis=0,
            )
            keys = jnp.concatenate([k_prev[base:, cols], k_ref[: base + rows, cols]], axis=0)
            vals = jnp.concatenate([v_prev[base:, cols], v_ref[: base + rows, cols]], axis=0)
            score = lax.dot_general(q, keys, dims, preferred_element_type=jnp.float32)
            bias = jnp.where(window_col >= before, band_bias[g], NEG)
            score = score.reshape(group, rows, span) + bias[None]
            top = jnp.max(score, axis=-1, keepdims=True)
            weight = jnp.exp2((score - top) * factor)
            win_top[tile, g] = top.reshape(group * rows, 1)
            win_total[tile, g] = jnp.sum(weight, axis=-1, keepdims=True).reshape(group * rows, 1)
            win_out[tile, g] = jnp.dot(
                weight.astype(jnp.bfloat16).reshape(group * rows, span),
                vals,
                preferred_element_type=jnp.float32,
            )

    each(n_z, lambda i: relay_arrival(i).wait_recv())

    vert_k, vert_v, vert_pos = [], [], []
    for g in range(heads):
        owners = [lax.div(vert_ref[g, j], per_shard) for j in range(slots)]
        vert_k.append(jnp.concatenate([gath[o, g, 0] for o in owners], axis=0))
        vert_v.append(jnp.concatenate([gath[o, g, 1] for o in owners], axis=0))
        first = jnp.zeros_like(vert_lane)
        for j in range(slots):
            first = jnp.where(vert_lane // BLK == j, vert_ref[g, j], first)
        vert_pos.append(first * BLK + vert_lane % BLK)

    half = n_kvh // 2
    for turn in range(n_kvh):
        tile = lax.rem(half * (1 - me // half) + turn, n_kvh)
        base = pl.multiple_of(tile * rows, rows)
        for g in range(heads):
            q = jnp.concatenate(
                [
                    q_ref[pl.ds(base, rows), (g * group + h) * hd : (g * group + h + 1) * hd]
                    for h in range(group)
                ],
                axis=0,
            )
            score = lax.dot_general(q, vert_k[g], dims, preferred_element_type=jnp.float32)
            vert_lag = vert_row + (c * tok + base) - vert_pos[g]
            mask = (vert_lag >= 0) & ~in_bands(vert_lag, g)
            score = jnp.where(mask[None], score.reshape(group, rows, slots * BLK), NEG)
            score = score.reshape(group * rows, slots * BLK)
            before_top = win_top[tile, g]
            top = jnp.maximum(before_top, jnp.max(score, axis=-1, keepdims=True))
            weight = jnp.exp2((score - top) * factor)
            fade = jnp.exp2((before_top - top) * factor)
            total = win_total[tile, g] * fade + jnp.sum(weight, axis=-1, keepdims=True)
            blended = win_out[tile, g] * fade + jnp.dot(
                weight.astype(jnp.bfloat16), vert_v[g], preferred_element_type=jnp.float32
            )
            result = (blended / total).astype(jnp.bfloat16)
            for h in range(group):
                obuf[pl.ds(base, rows), (g * group + h) * hd : (g * group + h + 1) * hd] = result[
                    h * rows : (h + 1) * rows
                ]

            @pl.when(tile != me)
            def _():
                out_copy(tile, g).start()

            @pl.when(tile == me)
            def _():
                out_own(tile, g).start()

    each(n_z - 1, lambda i: column_copy(i).wait_send())
    each(n_z, lambda i: relay_copy(i).wait_send())
    for chunk in range(n_kvh):
        for which in range(2):

            @pl.when((x == 0) | odd_sends)
            def _():
                kv_copy(which, chunk).wait_send()

            @pl.when(relays[which])
            def _():
                onward_copy(which, chunk).wait_send()

    for peer in range(n_kvh):
        for g in range(heads):

            @pl.when(peer != me)
            def _():
                out_copy(peer, g).wait_send()
                out_arrival(peer, g).wait_recv()

            @pl.when(peer == me)
            def _():
                out_own(peer, g).wait()


def per_device(n_ctx, n_kvh, queries, keys, values, vertical, offsets):
    tok = queries.shape[0]
    heads = vertical.shape[0]
    hd = keys.shape[1] // heads
    rows = tok // n_kvh
    group = queries.shape[1] // keys.shape[1]
    hbm = pl.BlockSpec(memory_space=pltpu.HBM)
    dma = pltpu.SemaphoreType.DMA
    return pl.pallas_call(
        functools.partial(kernel, n_ctx, n_kvh),
        out_shape=jax.ShapeDtypeStruct((rows, queries.shape[1] * n_kvh), jnp.bfloat16),
        in_specs=[hbm] * 5,
        out_specs=pl.BlockSpec(memory_space=pltpu.VMEM),
        scratch_shapes=[
            pltpu.SMEM(vertical.shape, jnp.int32),
            pltpu.SMEM(offsets.shape, jnp.int32),
            pltpu.VMEM(queries.shape, jnp.bfloat16),
            pltpu.VMEM(keys.shape, jnp.bfloat16),
            pltpu.VMEM(values.shape, jnp.bfloat16),
            pltpu.VMEM(keys.shape, jnp.bfloat16),
            pltpu.VMEM(values.shape, jnp.bfloat16),
            pltpu.VMEM((n_ctx, heads, 2, BLK, hd), jnp.bfloat16),
            pltpu.VMEM(queries.shape, jnp.bfloat16),
            dma((2, n_kvh)),
            dma((2, n_kvh)),
            dma((n_ctx // 2,)),
            dma((n_ctx // 2,)),
            dma((n_ctx // 2,)),
            dma((n_ctx // 2,)),
            dma((n_kvh, heads)),
            dma((n_kvh, heads)),
            dma((heads,)),
            dma((5,)),
            pltpu.VMEM((heads, rows, rows + tok), jnp.float32),
            pltpu.VMEM((n_kvh, heads, group * rows, 1), jnp.float32),
            pltpu.VMEM((n_kvh, heads, group * rows, 1), jnp.float32),
            pltpu.VMEM((n_kvh, heads, group * rows, hd), jnp.float32),
            pltpu.VMEM(keys.shape, jnp.bfloat16),
            dma((n_kvh,)),
            dma((n_kvh,)),
        ],
        compiler_params=pltpu.CompilerParams(
            collective_id=0, has_side_effects=True, vmem_limit_bytes=64 * 1024 * 1024
        ),
    )(vertical, offsets, queries, keys, values)


def solution(mesh):
    placed = (P("ctx", "kvh"), P("ctx", "kvh"), P("ctx", "kvh"), P("kvh", None), P("kvh", None))
    return jax.shard_map(
        functools.partial(per_device, mesh.shape["ctx"], mesh.shape["kvh"]),
        mesh=mesh,
        in_specs=placed,
        out_specs=P(("ctx", "kvh"), None),
        check_vma=False,
    )
```

```python
import functools
import math

import jax
import jax.numpy as jnp
from jax import lax
from jax.experimental import pallas as pl
from jax.experimental.pallas import tpu as pltpu
from jax.sharding import PartitionSpec as P

BLK = 64
NEG = -1e30
MESH = pl.DeviceIdType.MESH


def each(count, body):
    if count <= 16:
        for i in range(count):
            body(i)
    else:
        lax.fori_loop(0, count, lambda i, carry: (body(i), carry)[1], 0)


def kernel(
    n_ctx,
    n_kvh,
    vert_hbm,
    offs_hbm,
    q_hbm,
    k_hbm,
    v_hbm,
    out_ref,
    vert_ref,
    offs_ref,
    q_ref,
    k_ref,
    v_ref,
    k_prev,
    v_prev,
    gath,
    obuf,
    kv_send,
    kv_recv,
    vert_send,
    vert_recv,
    out_send,
    out_recv,
    out_local,
    load_sem,
    band_bias,
    win_top,
    win_total,
    win_out,
):
    c = lax.axis_index("ctx")
    me = lax.axis_index("kvh")
    tok = q_ref.shape[0]
    heads = vert_ref.shape[0]
    slots = vert_ref.shape[1]
    bands = offs_ref.shape[1]
    hd = k_ref.shape[1] // heads
    group = q_ref.shape[1] // k_ref.shape[1]
    gcols = group * hd
    rows = tok // n_kvh
    span = rows + tok
    per_shard = tok // BLK

    def ctx_peer(i):
        return lax.rem(c + 1 + i, n_ctx)

    loads = [
        pltpu.make_async_copy(src, dst, load_sem.at[i])
        for i, (src, dst) in enumerate(
            (
                (vert_hbm, vert_ref),
                (offs_hbm, offs_ref),
                (k_hbm, k_ref),
                (v_hbm, v_ref),
                (q_hbm, q_ref),
            )
        )
    ]
    for load in loads:
        load.start()

    barrier = pltpu.get_barrier_semaphore()
    each(
        n_ctx - 1,
        lambda i: pl.semaphore_signal(
            barrier, inc=1, device_id={"ctx": ctx_peer(i)}, device_id_type=MESH
        ),
    )
    for i in range(n_kvh - 1):
        pl.semaphore_signal(
            barrier,
            inc=1,
            device_id={"kvh": lax.rem(me + 1 + i, n_kvh)},
            device_id_type=MESH,
        )

    for load in loads[:4]:
        load.wait()

    for g in range(heads):
        row = jnp.int32(0)
        for j in range(slots):
            block = vert_ref[g, j]
            away = lax.div(block, per_shard) - c
            row = row + lax.rem(block, per_shard) * (1 - jnp.minimum(away * away, 1))
        row = row * BLK
        cols = slice(g * hd, (g + 1) * hd)
        gath[c, g, 0] = k_ref[pl.ds(row, BLK), cols]
        gath[c, g, 1] = v_ref[pl.ds(row, BLK), cols]

    pl.semaphore_wait(barrier, n_ctx - 1 + n_kvh - 1)

    def vert_copy(i):
        peer = ctx_peer(i)
        return pltpu.make_async_remote_copy(
            src_ref=gath.at[c],
            dst_ref=gath.at[c],
            send_sem=vert_send.at[peer],
            recv_sem=vert_recv.at[c],
            device_id={"ctx": peer},
            device_id_type=MESH,
        )

    def vert_arrival(i):
        peer = ctx_peer(i)
        return pltpu.make_async_remote_copy(
            src_ref=gath.at[peer],
            dst_ref=gath.at[peer],
            send_sem=vert_send.at[peer],
            recv_sem=vert_recv.at[peer],
            device_id={"ctx": peer},
            device_id_type=MESH,
        )

    def kv_copy(which, chunk):
        src, dst = ((k_hbm, k_prev), (v_hbm, v_prev))[which]
        part = pl.ds(chunk * rows, rows)
        return pltpu.make_async_remote_copy(
            src_ref=src.at[part],
            dst_ref=dst.at[part],
            send_sem=kv_send.at[which, chunk],
            recv_sem=kv_recv.at[which, chunk],
            device_id={"ctx": lax.rem(c + 1, n_ctx)},
            device_id_type=MESH,
        )

    each(n_ctx - 1, lambda i: vert_copy(i).start())

    @pl.when(c < n_ctx - 1)
    def _():
        for chunk in reversed(range(n_kvh)):
            for which in range(2):
                kv_copy(which, chunk).start()

    @pl.when(c == 0)
    def _():
        k_prev[...] = jnp.zeros_like(k_prev)
        v_prev[...] = jnp.zeros_like(v_prev)

    lag = (
        lax.broadcasted_iota(jnp.int32, (rows, span), 0)
        + tok
        - lax.broadcasted_iota(jnp.int32, (rows, span), 1)
    )
    window_col = lax.broadcasted_iota(jnp.int32, (rows, span), 1)
    vert_lane = lax.broadcasted_iota(jnp.int32, (1, slots * BLK), 1)
    vert_row = lax.broadcasted_iota(jnp.int32, (rows, slots * BLK), 0)

    def in_bands(distance, g):
        found = None
        for s in range(bands):
            gap = distance - offs_ref[g, s]
            hit = (gap >= 0) & (gap < BLK)
            found = hit if found is None else found | hit
        return found

    for g in range(heads):
        band_bias[g] = jnp.where(in_bands(lag, g), 0.0, NEG)
    loads[4].wait()

    factor = math.log2(math.e) * hd**-0.5

    def out_copy(tile, g):
        return pltpu.make_async_remote_copy(
            src_ref=obuf.at[pl.ds(tile * rows, rows), pl.ds(g * gcols, gcols)],
            dst_ref=out_ref.at[
                :, pl.ds(pl.multiple_of(me * heads * gcols + g * gcols, gcols), gcols)
            ],
            send_sem=out_send.at[tile, g],
            recv_sem=out_recv.at[me, g],
            device_id={"kvh": tile},
            device_id_type=MESH,
        )

    def out_own(tile, g):
        return pltpu.make_async_copy(
            obuf.at[pl.ds(tile * rows, rows), pl.ds(g * gcols, gcols)],
            out_ref.at[
                :, pl.ds(pl.multiple_of(me * heads * gcols + g * gcols, gcols), gcols)
            ],
            out_local.at[g],
        )

    def out_arrival(peer, g):
        return pltpu.make_async_remote_copy(
            src_ref=obuf.at[pl.ds(0, rows), pl.ds(g * gcols, gcols)],
            dst_ref=out_ref.at[:, pl.ds(peer * heads * gcols + g * gcols, gcols)],
            send_sem=out_send.at[peer, g],
            recv_sem=out_recv.at[peer, g],
            device_id={"kvh": peer},
            device_id_type=MESH,
        )

    dims = (((1,), (1,)), ((), ()))

    for tile in reversed(range(n_kvh)):
        base = tile * rows

        @pl.when(c > 0)
        def _():
            for which in range(2):
                kv_copy(which, tile).wait_recv()

        before = jnp.where(c == 0, tok - base, 0)
        for g in range(heads):
            cols = slice(g * hd, (g + 1) * hd)
            q = jnp.concatenate(
                [
                    q_ref[base : base + rows, (g * group + h) * hd : (g * group + h + 1) * hd]
                    for h in range(group)
                ],
                axis=0,
            )
            keys = jnp.concatenate([k_prev[base:, cols], k_ref[: base + rows, cols]], axis=0)
            vals = jnp.concatenate([v_prev[base:, cols], v_ref[: base + rows, cols]], axis=0)
            score = lax.dot_general(q, keys, dims, preferred_element_type=jnp.float32)
            bias = jnp.where(window_col >= before, band_bias[g], NEG)
            score = score.reshape(group, rows, span) + bias[None]
            top = jnp.max(score, axis=-1, keepdims=True)
            weight = jnp.exp2((score - top) * factor)
            win_top[tile, g] = top.reshape(group * rows, 1)
            win_total[tile, g] = jnp.sum(weight, axis=-1, keepdims=True).reshape(group * rows, 1)
            win_out[tile, g] = jnp.dot(
                weight.astype(jnp.bfloat16).reshape(group * rows, span),
                vals,
                preferred_element_type=jnp.float32,
            )

    each(n_ctx - 1, lambda i: vert_arrival(i).wait_recv())

    vert_k, vert_v, vert_pos = [], [], []
    for g in range(heads):
        owners = [lax.div(vert_ref[g, j], per_shard) for j in range(slots)]
        vert_k.append(jnp.concatenate([gath[o, g, 0] for o in owners], axis=0))
        vert_v.append(jnp.concatenate([gath[o, g, 1] for o in owners], axis=0))
        first = jnp.zeros_like(vert_lane)
        for j in range(slots):
            first = jnp.where(vert_lane // BLK == j, vert_ref[g, j], first)
        vert_pos.append(first * BLK + vert_lane % BLK)

    half = n_kvh // 2
    for turn in range(n_kvh):
        tile = lax.rem(half * (1 - me // half) + turn, n_kvh)
        base = pl.multiple_of(tile * rows, rows)
        for g in range(heads):
            q = jnp.concatenate(
                [
                    q_ref[pl.ds(base, rows), (g * group + h) * hd : (g * group + h + 1) * hd]
                    for h in range(group)
                ],
                axis=0,
            )
            score = lax.dot_general(q, vert_k[g], dims, preferred_element_type=jnp.float32)
            vert_lag = vert_row + (c * tok + base) - vert_pos[g]
            mask = (vert_lag >= 0) & ~in_bands(vert_lag, g)
            score = jnp.where(mask[None], score.reshape(group, rows, slots * BLK), NEG)
            score = score.reshape(group * rows, slots * BLK)
            before_top = win_top[tile, g]
            top = jnp.maximum(before_top, jnp.max(score, axis=-1, keepdims=True))
            weight = jnp.exp2((score - top) * factor)
            fade = jnp.exp2((before_top - top) * factor)
            total = win_total[tile, g] * fade + jnp.sum(weight, axis=-1, keepdims=True)
            blended = win_out[tile, g] * fade + jnp.dot(
                weight.astype(jnp.bfloat16), vert_v[g], preferred_element_type=jnp.float32
            )
            result = (blended / total).astype(jnp.bfloat16)
            for h in range(group):
                obuf[pl.ds(base, rows), (g * group + h) * hd : (g * group + h + 1) * hd] = result[
                    h * rows : (h + 1) * rows
                ]

            @pl.when(tile != me)
            def _():
                out_copy(tile, g).start()

            @pl.when(tile == me)
            def _():
                out_own(tile, g).start()

    each(n_ctx - 1, lambda i: vert_copy(i).wait_send())

    @pl.when(c < n_ctx - 1)
    def _():
        for chunk in range(n_kvh):
            for which in range(2):
                kv_copy(which, chunk).wait_send()

    for peer in range(n_kvh):
        for g in range(heads):

            @pl.when(peer != me)
            def _():
                out_copy(peer, g).wait_send()
                out_arrival(peer, g).wait_recv()

            @pl.when(peer == me)
            def _():
                out_own(peer, g).wait()


def per_device(n_ctx, n_kvh, queries, keys, values, vertical, offsets):
    tok = queries.shape[0]
    heads = vertical.shape[0]
    hd = keys.shape[1] // heads
    rows = tok // n_kvh
    group = queries.shape[1] // keys.shape[1]
    hbm = pl.BlockSpec(memory_space=pltpu.HBM)
    dma = pltpu.SemaphoreType.DMA
    return pl.pallas_call(
        functools.partial(kernel, n_ctx, n_kvh),
        out_shape=jax.ShapeDtypeStruct((rows, queries.shape[1] * n_kvh), jnp.bfloat16),
        in_specs=[hbm] * 5,
        out_specs=pl.BlockSpec(memory_space=pltpu.VMEM),
        scratch_shapes=[
            pltpu.SMEM(vertical.shape, jnp.int32),
            pltpu.SMEM(offsets.shape, jnp.int32),
            pltpu.VMEM(queries.shape, jnp.bfloat16),
            pltpu.VMEM(keys.shape, jnp.bfloat16),
            pltpu.VMEM(values.shape, jnp.bfloat16),
            pltpu.VMEM(keys.shape, jnp.bfloat16),
            pltpu.VMEM(values.shape, jnp.bfloat16),
            pltpu.VMEM((n_ctx, heads, 2, BLK, hd), jnp.bfloat16),
            pltpu.VMEM(queries.shape, jnp.bfloat16),
            dma((2, n_kvh)),
            dma((2, n_kvh)),
            dma((n_ctx,)),
            dma((n_ctx,)),
            dma((n_kvh, heads)),
            dma((n_kvh, heads)),
            dma((heads,)),
            dma((5,)),
            pltpu.VMEM((heads, rows, rows + tok), jnp.float32),
            pltpu.VMEM((n_kvh, heads, group * rows, 1), jnp.float32),
            pltpu.VMEM((n_kvh, heads, group * rows, 1), jnp.float32),
            pltpu.VMEM((n_kvh, heads, group * rows, hd), jnp.float32),
        ],
        compiler_params=pltpu.CompilerParams(
            collective_id=0, has_side_effects=True, vmem_limit_bytes=64 * 1024 * 1024
        ),
    )(vertical, offsets, queries, keys, values)


def solution(mesh):
    placed = (P("ctx", "kvh"), P("ctx", "kvh"), P("ctx", "kvh"), P("kvh", None), P("kvh", None))
    return jax.shard_map(
        functools.partial(per_device, mesh.shape["ctx"], mesh.shape["kvh"]),
        mesh=mesh,
        in_specs=placed,
        out_specs=P(("ctx", "kvh"), None),
        check_vma=False,
    )
```

```python
import functools
import math

import jax
import jax.numpy as jnp
from jax import lax
from jax.experimental import pallas as pl
from jax.experimental.pallas import tpu as pltpu
from jax.sharding import PartitionSpec as P

BLK = 64
NEG = -1e30
MESH = pl.DeviceIdType.MESH


def each(count, body):
    if count <= 16:
        for i in range(count):
            body(i)
    else:
        lax.fori_loop(0, count, lambda i, carry: (body(i), carry)[1], 0)


def kernel(
    n_ctx,
    n_kvh,
    vert_hbm,
    offs_hbm,
    q_hbm,
    k_hbm,
    v_hbm,
    out_ref,
    vert_ref,
    offs_ref,
    q_ref,
    k_ref,
    v_ref,
    k_prev,
    v_prev,
    gath,
    obuf,
    kv_send,
    kv_recv,
    vert_send,
    vert_recv,
    out_send,
    out_recv,
    out_local,
    load_sem,
    band_bias,
):
    c = lax.axis_index("ctx")
    me = lax.axis_index("kvh")
    tok = q_ref.shape[0]
    heads = vert_ref.shape[0]
    slots = vert_ref.shape[1]
    bands = offs_ref.shape[1]
    hd = k_ref.shape[1] // heads
    group = q_ref.shape[1] // k_ref.shape[1]
    gcols = group * hd
    rows = tok // n_kvh
    span = rows + tok
    per_shard = tok // BLK

    def ctx_peer(i):
        return lax.rem(c + 1 + i, n_ctx)

    loads = [
        pltpu.make_async_copy(src, dst, load_sem.at[i])
        for i, (src, dst) in enumerate(
            (
                (vert_hbm, vert_ref),
                (offs_hbm, offs_ref),
                (k_hbm, k_ref),
                (v_hbm, v_ref),
                (q_hbm, q_ref),
            )
        )
    ]
    for load in loads:
        load.start()

    barrier = pltpu.get_barrier_semaphore()
    each(
        n_ctx - 1,
        lambda i: pl.semaphore_signal(
            barrier, inc=1, device_id={"ctx": ctx_peer(i)}, device_id_type=MESH
        ),
    )
    for i in range(n_kvh - 1):
        pl.semaphore_signal(
            barrier,
            inc=1,
            device_id={"kvh": lax.rem(me + 1 + i, n_kvh)},
            device_id_type=MESH,
        )

    for load in loads[:4]:
        load.wait()

    for g in range(heads):
        row = jnp.int32(0)
        for j in range(slots):
            block = vert_ref[g, j]
            away = lax.div(block, per_shard) - c
            row = row + lax.rem(block, per_shard) * (1 - jnp.minimum(away * away, 1))
        row = row * BLK
        cols = slice(g * hd, (g + 1) * hd)
        gath[c, g, 0] = k_ref[pl.ds(row, BLK), cols]
        gath[c, g, 1] = v_ref[pl.ds(row, BLK), cols]

    pl.semaphore_wait(barrier, n_ctx - 1 + n_kvh - 1)

    def vert_copy(i):
        peer = ctx_peer(i)
        return pltpu.make_async_remote_copy(
            src_ref=gath.at[c],
            dst_ref=gath.at[c],
            send_sem=vert_send.at[peer],
            recv_sem=vert_recv.at[c],
            device_id={"ctx": peer},
            device_id_type=MESH,
        )

    def vert_arrival(i):
        peer = ctx_peer(i)
        return pltpu.make_async_remote_copy(
            src_ref=gath.at[peer],
            dst_ref=gath.at[peer],
            send_sem=vert_send.at[peer],
            recv_sem=vert_recv.at[peer],
            device_id={"ctx": peer},
            device_id_type=MESH,
        )

    def kv_copy(which, chunk):
        src, dst = ((k_hbm, k_prev), (v_hbm, v_prev))[which]
        part = pl.ds(chunk * rows, rows)
        return pltpu.make_async_remote_copy(
            src_ref=src.at[part],
            dst_ref=dst.at[part],
            send_sem=kv_send.at[which, chunk],
            recv_sem=kv_recv.at[which, chunk],
            device_id={"ctx": lax.rem(c + 1, n_ctx)},
            device_id_type=MESH,
        )

    each(n_ctx - 1, lambda i: vert_copy(i).start())

    @pl.when(c < n_ctx - 1)
    def _():
        for chunk in reversed(range(n_kvh)):
            for which in range(2):
                kv_copy(which, chunk).start()

    @pl.when(c == 0)
    def _():
        k_prev[...] = jnp.zeros_like(k_prev)
        v_prev[...] = jnp.zeros_like(v_prev)

    lag = (
        lax.broadcasted_iota(jnp.int32, (rows, span), 0)
        + tok
        - lax.broadcasted_iota(jnp.int32, (rows, span), 1)
    )
    window_col = lax.broadcasted_iota(jnp.int32, (rows, span), 1)
    vert_lane = lax.broadcasted_iota(jnp.int32, (1, slots * BLK), 1)
    vert_row = lax.broadcasted_iota(jnp.int32, (rows, slots * BLK), 0)

    def in_bands(distance, g):
        found = None
        for s in range(bands):
            gap = distance - offs_ref[g, s]
            hit = (gap >= 0) & (gap < BLK)
            found = hit if found is None else found | hit
        return found

    for g in range(heads):
        band_bias[g] = jnp.where(in_bands(lag, g), 0.0, NEG)
    loads[4].wait()

    each(n_ctx - 1, lambda i: vert_arrival(i).wait_recv())

    vert_k, vert_v, vert_pos = [], [], []
    for g in range(heads):
        owners = [lax.div(vert_ref[g, j], per_shard) for j in range(slots)]
        vert_k.append(jnp.concatenate([gath[o, g, 0] for o in owners], axis=0))
        vert_v.append(jnp.concatenate([gath[o, g, 1] for o in owners], axis=0))
        first = jnp.zeros_like(vert_lane)
        for j in range(slots):
            first = jnp.where(vert_lane // BLK == j, vert_ref[g, j], first)
        vert_pos.append(first * BLK + vert_lane % BLK)

    factor = math.log2(math.e) * hd**-0.5

    def out_copy(tile, g):
        return pltpu.make_async_remote_copy(
            src_ref=obuf.at[pl.ds(tile * rows, rows), pl.ds(g * gcols, gcols)],
            dst_ref=out_ref.at[
                :, pl.ds(pl.multiple_of(me * heads * gcols + g * gcols, gcols), gcols)
            ],
            send_sem=out_send.at[tile, g],
            recv_sem=out_recv.at[me, g],
            device_id={"kvh": tile},
            device_id_type=MESH,
        )

    def out_own(tile, g):
        return pltpu.make_async_copy(
            obuf.at[pl.ds(tile * rows, rows), pl.ds(g * gcols, gcols)],
            out_ref.at[
                :, pl.ds(pl.multiple_of(me * heads * gcols + g * gcols, gcols), gcols)
            ],
            out_local.at[g],
        )

    def out_arrival(peer, g):
        return pltpu.make_async_remote_copy(
            src_ref=obuf.at[pl.ds(0, rows), pl.ds(g * gcols, gcols)],
            dst_ref=out_ref.at[:, pl.ds(peer * heads * gcols + g * gcols, gcols)],
            send_sem=out_send.at[peer, g],
            recv_sem=out_recv.at[peer, g],
            device_id={"kvh": peer},
            device_id_type=MESH,
        )

    for tile in reversed(range(n_kvh)):
        base = tile * rows

        @pl.when(c > 0)
        def _():
            for which in range(2):
                kv_copy(which, tile).wait_recv()

        before = jnp.where(c == 0, tok - base, 0)
        for g in range(heads):
            cols = slice(g * hd, (g + 1) * hd)
            q = jnp.concatenate(
                [
                    q_ref[base : base + rows, (g * group + h) * hd : (g * group + h + 1) * hd]
                    for h in range(group)
                ],
                axis=0,
            )
            keys = jnp.concatenate([k_prev[base:, cols], k_ref[: base + rows, cols]], axis=0)
            vals = jnp.concatenate([v_prev[base:, cols], v_ref[: base + rows, cols]], axis=0)
            dims = (((1,), (1,)), ((), ()))
            score_w = lax.dot_general(q, keys, dims, preferred_element_type=jnp.float32)
            score_v = lax.dot_general(q, vert_k[g], dims, preferred_element_type=jnp.float32)
            bias_w = jnp.where(window_col >= before, band_bias[g], NEG)
            vert_lag = vert_row + (c * tok + base) - vert_pos[g]
            mask_v = (vert_lag >= 0) & ~in_bands(vert_lag, g)
            score_w = score_w.reshape(group, rows, span) + bias_w[None]
            score_v = jnp.where(mask_v[None], score_v.reshape(group, rows, slots * BLK), NEG)
            top = jnp.maximum(
                jnp.max(score_w, axis=-1, keepdims=True), jnp.max(score_v, axis=-1, keepdims=True)
            )
            exp_w = jnp.exp2((score_w - top) * factor)
            exp_v = jnp.exp2((score_v - top) * factor)
            blended = jnp.dot(
                exp_w.astype(jnp.bfloat16).reshape(group * rows, span),
                jnp.concatenate([vals, jnp.ones_like(vals)], axis=1),
                preferred_element_type=jnp.float32,
            ) + jnp.dot(
                exp_v.astype(jnp.bfloat16).reshape(group * rows, slots * BLK),
                jnp.concatenate([vert_v[g], jnp.ones_like(vert_v[g])], axis=1),
                preferred_element_type=jnp.float32,
            )
            result = (blended[:, :hd] / blended[:, hd:]).astype(jnp.bfloat16)
            result = result.reshape(group, rows, hd)
            for h in range(group):
                obuf[base : base + rows, (g * group + h) * hd : (g * group + h + 1) * hd] = result[h]

            @pl.when(tile != me)
            def _():
                out_copy(tile, g).start()

            @pl.when(tile == me)
            def _():
                out_own(tile, g).start()

    each(n_ctx - 1, lambda i: vert_copy(i).wait_send())

    @pl.when(c < n_ctx - 1)
    def _():
        for chunk in range(n_kvh):
            for which in range(2):
                kv_copy(which, chunk).wait_send()

    for peer in range(n_kvh):
        for g in range(heads):

            @pl.when(peer != me)
            def _():
                out_copy(peer, g).wait_send()
                out_arrival(peer, g).wait_recv()

            @pl.when(peer == me)
            def _():
                out_own(peer, g).wait()


def per_device(n_ctx, n_kvh, queries, keys, values, vertical, offsets):
    tok = queries.shape[0]
    heads = vertical.shape[0]
    hd = keys.shape[1] // heads
    rows = tok // n_kvh
    hbm = pl.BlockSpec(memory_space=pltpu.HBM)
    dma = pltpu.SemaphoreType.DMA
    return pl.pallas_call(
        functools.partial(kernel, n_ctx, n_kvh),
        out_shape=jax.ShapeDtypeStruct((rows, queries.shape[1] * n_kvh), jnp.bfloat16),
        in_specs=[hbm] * 5,
        out_specs=pl.BlockSpec(memory_space=pltpu.VMEM),
        scratch_shapes=[
            pltpu.SMEM(vertical.shape, jnp.int32),
            pltpu.SMEM(offsets.shape, jnp.int32),
            pltpu.VMEM(queries.shape, jnp.bfloat16),
            pltpu.VMEM(keys.shape, jnp.bfloat16),
            pltpu.VMEM(values.shape, jnp.bfloat16),
            pltpu.VMEM(keys.shape, jnp.bfloat16),
            pltpu.VMEM(values.shape, jnp.bfloat16),
            pltpu.VMEM((n_ctx, heads, 2, BLK, hd), jnp.bfloat16),
            pltpu.VMEM(queries.shape, jnp.bfloat16),
            dma((2, n_kvh)),
            dma((2, n_kvh)),
            dma((n_ctx,)),
            dma((n_ctx,)),
            dma((n_kvh, heads)),
            dma((n_kvh, heads)),
            dma((heads,)),
            dma((5,)),
            pltpu.VMEM((heads, rows, rows + tok), jnp.float32),
        ],
        compiler_params=pltpu.CompilerParams(
            collective_id=0, has_side_effects=True, vmem_limit_bytes=64 * 1024 * 1024
        ),
    )(vertical, offsets, queries, keys, values)


def solution(mesh):
    placed = (P("ctx", "kvh"), P("ctx", "kvh"), P("ctx", "kvh"), P("kvh", None), P("kvh", None))
    return jax.shard_map(
        functools.partial(per_device, mesh.shape["ctx"], mesh.shape["kvh"]),
        mesh=mesh,
        in_specs=placed,
        out_specs=P(("ctx", "kvh"), None),
        check_vma=False,
    )
```

```python
import functools
import math

import jax
import jax.numpy as jnp
from jax import lax
from jax.experimental import pallas as pl
from jax.experimental.pallas import tpu as pltpu
from jax.sharding import PartitionSpec as P

BLK = 64
NEG = -1e30
MESH = pl.DeviceIdType.MESH


def each(count, body):
    if count <= 16:
        for i in range(count):
            body(i)
    else:
        lax.fori_loop(0, count, lambda i, carry: (body(i), carry)[1], 0)


def kernel(
    n_ctx,
    n_kvh,
    vert_hbm,
    offs_hbm,
    q_hbm,
    k_hbm,
    v_hbm,
    out_ref,
    vert_ref,
    offs_ref,
    q_ref,
    k_ref,
    v_ref,
    k_prev,
    v_prev,
    gath,
    obuf,
    kv_send,
    kv_recv,
    vert_send,
    vert_recv,
    out_send,
    out_recv,
    out_local,
    load_sem,
    band_bias,
):
    c = lax.axis_index("ctx")
    me = lax.axis_index("kvh")
    tok = q_ref.shape[0]
    heads = vert_ref.shape[0]
    slots = vert_ref.shape[1]
    bands = offs_ref.shape[1]
    hd = k_ref.shape[1] // heads
    group = q_ref.shape[1] // k_ref.shape[1]
    gcols = group * hd
    rows = tok // n_kvh
    span = rows + tok
    per_shard = tok // BLK

    def ctx_peer(i):
        return lax.rem(c + 1 + i, n_ctx)

    loads = [
        pltpu.make_async_copy(src, dst, load_sem.at[i])
        for i, (src, dst) in enumerate(
            (
                (vert_hbm, vert_ref),
                (offs_hbm, offs_ref),
                (k_hbm, k_ref),
                (v_hbm, v_ref),
                (q_hbm, q_ref),
            )
        )
    ]
    for load in loads:
        load.start()

    barrier = pltpu.get_barrier_semaphore()
    each(
        n_ctx - 1,
        lambda i: pl.semaphore_signal(
            barrier, inc=1, device_id={"ctx": ctx_peer(i)}, device_id_type=MESH
        ),
    )
    for i in range(n_kvh - 1):
        pl.semaphore_signal(
            barrier,
            inc=1,
            device_id={"kvh": lax.rem(me + 1 + i, n_kvh)},
            device_id_type=MESH,
        )

    for load in loads[:4]:
        load.wait()

    for g in range(heads):
        row = jnp.int32(0)
        for j in range(slots):
            block = vert_ref[g, j]
            away = lax.div(block, per_shard) - c
            row = row + lax.rem(block, per_shard) * (1 - jnp.minimum(away * away, 1))
        row = row * BLK
        cols = slice(g * hd, (g + 1) * hd)
        gath[c, g, 0] = k_ref[pl.ds(row, BLK), cols]
        gath[c, g, 1] = v_ref[pl.ds(row, BLK), cols]

    pl.semaphore_wait(barrier, n_ctx - 1 + n_kvh - 1)

    def vert_copy(i):
        peer = ctx_peer(i)
        return pltpu.make_async_remote_copy(
            src_ref=gath.at[c],
            dst_ref=gath.at[c],
            send_sem=vert_send.at[peer],
            recv_sem=vert_recv.at[c],
            device_id={"ctx": peer},
            device_id_type=MESH,
        )

    def vert_arrival(i):
        peer = ctx_peer(i)
        return pltpu.make_async_remote_copy(
            src_ref=gath.at[peer],
            dst_ref=gath.at[peer],
            send_sem=vert_send.at[peer],
            recv_sem=vert_recv.at[peer],
            device_id={"ctx": peer},
            device_id_type=MESH,
        )

    def kv_copy(which, chunk):
        src, dst = ((k_hbm, k_prev), (v_hbm, v_prev))[which]
        part = pl.ds(chunk * rows, rows)
        return pltpu.make_async_remote_copy(
            src_ref=src.at[part],
            dst_ref=dst.at[part],
            send_sem=kv_send.at[which, chunk],
            recv_sem=kv_recv.at[which, chunk],
            device_id={"ctx": lax.rem(c + 1, n_ctx)},
            device_id_type=MESH,
        )

    each(n_ctx - 1, lambda i: vert_copy(i).start())

    @pl.when(c < n_ctx - 1)
    def _():
        for chunk in reversed(range(n_kvh)):
            for which in range(2):
                kv_copy(which, chunk).start()

    @pl.when(c == 0)
    def _():
        k_prev[...] = jnp.zeros_like(k_prev)
        v_prev[...] = jnp.zeros_like(v_prev)

    lag = (
        lax.broadcasted_iota(jnp.int32, (rows, span), 0)
        + tok
        - lax.broadcasted_iota(jnp.int32, (rows, span), 1)
    )
    window_col = lax.broadcasted_iota(jnp.int32, (rows, span), 1)
    vert_lane = lax.broadcasted_iota(jnp.int32, (1, slots * BLK), 1)
    vert_row = lax.broadcasted_iota(jnp.int32, (rows, slots * BLK), 0)

    def in_bands(distance, g):
        found = None
        for s in range(bands):
            gap = distance - offs_ref[g, s]
            hit = (gap >= 0) & (gap < BLK)
            found = hit if found is None else found | hit
        return found

    for g in range(heads):
        band_bias[g] = jnp.where(in_bands(lag, g), 0.0, NEG)
    loads[4].wait()

    each(n_ctx - 1, lambda i: vert_arrival(i).wait_recv())

    vert_k, vert_v, vert_pos = [], [], []
    for g in range(heads):
        owners = [lax.div(vert_ref[g, j], per_shard) for j in range(slots)]
        vert_k.append(jnp.concatenate([gath[o, g, 0] for o in owners], axis=0))
        vert_v.append(jnp.concatenate([gath[o, g, 1] for o in owners], axis=0))
        first = jnp.zeros_like(vert_lane)
        for j in range(slots):
            first = jnp.where(vert_lane // BLK == j, vert_ref[g, j], first)
        vert_pos.append(first * BLK + vert_lane % BLK)

    factor = math.log2(math.e) * hd**-0.5

    def out_copy(tile, g):
        return pltpu.make_async_remote_copy(
            src_ref=obuf.at[pl.ds(tile * rows, rows), pl.ds(g * gcols, gcols)],
            dst_ref=out_ref.at[
                :, pl.ds(pl.multiple_of(me * heads * gcols + g * gcols, gcols), gcols)
            ],
            send_sem=out_send.at[tile, g],
            recv_sem=out_recv.at[me, g],
            device_id={"kvh": tile},
            device_id_type=MESH,
        )

    def out_own(tile, g):
        return pltpu.make_async_copy(
            obuf.at[pl.ds(tile * rows, rows), pl.ds(g * gcols, gcols)],
            out_ref.at[
                :, pl.ds(pl.multiple_of(me * heads * gcols + g * gcols, gcols), gcols)
            ],
            out_local.at[g],
        )

    def out_arrival(peer, g):
        return pltpu.make_async_remote_copy(
            src_ref=obuf.at[pl.ds(0, rows), pl.ds(g * gcols, gcols)],
            dst_ref=out_ref.at[:, pl.ds(peer * heads * gcols + g * gcols, gcols)],
            send_sem=out_send.at[peer, g],
            recv_sem=out_recv.at[peer, g],
            device_id={"kvh": peer},
            device_id_type=MESH,
        )

    for tile in reversed(range(n_kvh)):
        base = tile * rows

        @pl.when(c > 0)
        def _():
            for which in range(2):
                kv_copy(which, tile).wait_recv()

        before = jnp.where(c == 0, tok - base, 0)
        for g in range(heads):
            cols = slice(g * hd, (g + 1) * hd)
            q = jnp.concatenate(
                [
                    q_ref[base : base + rows, (g * group + h) * hd : (g * group + h + 1) * hd]
                    for h in range(group)
                ],
                axis=0,
            )
            keys = jnp.concatenate([k_prev[base:, cols], k_ref[: base + rows, cols]], axis=0)
            vals = jnp.concatenate([v_prev[base:, cols], v_ref[: base + rows, cols]], axis=0)
            dims = (((1,), (1,)), ((), ()))
            score_w = lax.dot_general(q, keys, dims, preferred_element_type=jnp.float32)
            score_v = lax.dot_general(q, vert_k[g], dims, preferred_element_type=jnp.float32)
            bias_w = jnp.where(window_col >= before, band_bias[g], NEG)
            vert_lag = vert_row + (c * tok + base) - vert_pos[g]
            mask_v = (vert_lag >= 0) & ~in_bands(vert_lag, g)
            score_w = score_w.reshape(group, rows, span) + bias_w[None]
            score_v = jnp.where(mask_v[None], score_v.reshape(group, rows, slots * BLK), NEG)
            top = jnp.maximum(
                jnp.max(score_w, axis=-1, keepdims=True), jnp.max(score_v, axis=-1, keepdims=True)
            )
            exp_w = jnp.exp2((score_w - top) * factor)
            exp_v = jnp.exp2((score_v - top) * factor)
            total = jnp.sum(exp_w, axis=-1, keepdims=True) + jnp.sum(exp_v, axis=-1, keepdims=True)
            blended = jnp.dot(
                exp_w.astype(jnp.bfloat16).reshape(group * rows, span),
                vals,
                preferred_element_type=jnp.float32,
            ) + jnp.dot(
                exp_v.astype(jnp.bfloat16).reshape(group * rows, slots * BLK),
                vert_v[g],
                preferred_element_type=jnp.float32,
            )
            result = (blended.reshape(group, rows, hd) / total).astype(jnp.bfloat16)
            for h in range(group):
                obuf[base : base + rows, (g * group + h) * hd : (g * group + h + 1) * hd] = result[h]

            @pl.when(tile != me)
            def _():
                out_copy(tile, g).start()

            @pl.when(tile == me)
            def _():
                out_own(tile, g).start()

    each(n_ctx - 1, lambda i: vert_copy(i).wait_send())

    @pl.when(c < n_ctx - 1)
    def _():
        for chunk in range(n_kvh):
            for which in range(2):
                kv_copy(which, chunk).wait_send()

    for peer in range(n_kvh):
        for g in range(heads):

            @pl.when(peer != me)
            def _():
                out_copy(peer, g).wait_send()
                out_arrival(peer, g).wait_recv()

            @pl.when(peer == me)
            def _():
                out_own(peer, g).wait()


def per_device(n_ctx, n_kvh, queries, keys, values, vertical, offsets):
    tok = queries.shape[0]
    heads = vertical.shape[0]
    hd = keys.shape[1] // heads
    rows = tok // n_kvh
    hbm = pl.BlockSpec(memory_space=pltpu.HBM)
    dma = pltpu.SemaphoreType.DMA
    return pl.pallas_call(
        functools.partial(kernel, n_ctx, n_kvh),
        out_shape=jax.ShapeDtypeStruct((rows, queries.shape[1] * n_kvh), jnp.bfloat16),
        in_specs=[hbm] * 5,
        out_specs=hbm,
        scratch_shapes=[
            pltpu.SMEM(vertical.shape, jnp.int32),
            pltpu.SMEM(offsets.shape, jnp.int32),
            pltpu.VMEM(queries.shape, jnp.bfloat16),
            pltpu.VMEM(keys.shape, jnp.bfloat16),
            pltpu.VMEM(values.shape, jnp.bfloat16),
            pltpu.VMEM(keys.shape, jnp.bfloat16),
            pltpu.VMEM(values.shape, jnp.bfloat16),
            pltpu.VMEM((n_ctx, heads, 2, BLK, hd), jnp.bfloat16),
            pltpu.VMEM(queries.shape, jnp.bfloat16),
            dma((2, n_kvh)),
            dma((2, n_kvh)),
            dma((n_ctx,)),
            dma((n_ctx,)),
            dma((n_kvh, heads)),
            dma((n_kvh, heads)),
            dma((heads,)),
            dma((5,)),
            pltpu.VMEM((heads, rows, rows + tok), jnp.float32),
        ],
        compiler_params=pltpu.CompilerParams(
            collective_id=0, has_side_effects=True, vmem_limit_bytes=64 * 1024 * 1024
        ),
    )(vertical, offsets, queries, keys, values)


def solution(mesh):
    placed = (P("ctx", "kvh"), P("ctx", "kvh"), P("ctx", "kvh"), P("kvh", None), P("kvh", None))
    return jax.shard_map(
        functools.partial(per_device, mesh.shape["ctx"], mesh.shape["kvh"]),
        mesh=mesh,
        in_specs=placed,
        out_specs=P(("ctx", "kvh"), None),
        check_vma=False,
    )
```
